32 devices in a mesh: ctx: 16 (over z, x, core), head: 2 (over y).
Axes of the slice: x: 2, y: 2, z: 4, core: 2. Of those that a mesh axis runs over, the one named last changes fastest.
Arguments:
- absorbed_query: bfloat16 [64, 128, 576], P('ctx', 'head'), may hold values from -20 to 20
- index_query: bfloat16 [64, 64, 128], P('ctx', 'head'), may hold values from -20 to 20
- index_weight: bfloat16 [64, 64], P('ctx', 'head'), may hold values from -2 to 2
- kv_cache: bfloat16 [65536, 576], P('ctx'), may hold values from -4 to 4
- index_keys: bfloat16 [65536, 128], P('ctx'), may hold values from -4 to 4
- lengths: int32 [64], replicated, may hold values from 16384 to 65536
Outputs:
- target: float32 [64, 65536], P('head', 'ctx')
- gradient: float32 [64, 65536], P('head', 'ctx')
The draws below stay inside these ranges and needn't reach their ends.
All inputs are finite; a program needn't handle non-finite values.
Results may differ from the reference program's by a relative error of at most 0.0003.
Values may be sent and summed in bfloat16 or wider, within the bound.
No kernel may reach another device: no remote copies, remote signals or barrier semaphores. Data moves between devices by JAX's collectives and lax.ppermute only.
A program may use at most 192 MiB of HBM per device.

```python
import jax
import jax.numpy as jnp
from jax import lax

LATENT = 512
ROPE = 64
HEADS = 128
IDX_HEADS = 64
IDX_DIM = 128
ROWS = 64
KEYS = 65536


def key_spread(key):
    return jnp.exp(jax.random.uniform(key, (KEYS, 1), jnp.float32, -0.4, 0.4))


def cache_base(key):
    spread = key_spread(jax.random.fold_in(key, 121))
    base = jnp.clip(spread * jax.random.normal(jax.random.fold_in(key, 101), (KEYS, LATENT + ROPE), jnp.float32), -4.0, 4.0)
    return base


def index_base(key):
    spread = key_spread(jax.random.fold_in(key, 122))
    base = jnp.clip(spread * jax.random.normal(jax.random.fold_in(key, 102), (KEYS, IDX_DIM), jnp.float32), -4.0, 4.0)
    return base


def draw_kv_cache(key, part):
    return cache_base(key).astype(jnp.bfloat16)


def draw_index_keys(key, part):
    return index_base(key).astype(jnp.bfloat16)


def draw_absorbed_query(key, part):
    shared = jax.random.normal(jax.random.fold_in(key, 113), (ROWS, 1, LATENT + ROPE), jnp.float32)
    single = jax.random.normal(jax.random.fold_in(key, 103), (ROWS, HEADS, LATENT + ROPE), jnp.float32)
    values = jnp.clip(0.4 * shared + 0.7 * single, -3.2, 3.2)
    return values.astype(jnp.bfloat16)


def draw_index_query(key, part):
    values = jnp.clip(jax.random.normal(jax.random.fold_in(key, 105), (ROWS, IDX_HEADS, IDX_DIM), jnp.float32), -4.0, 4.0)
    return values.astype(jnp.bfloat16)


def place_ends(drawn, stream_key, low, top_value):
    place = [jax.random.randint(jax.random.fold_in(stream_key, axis), (), 0, length) for axis, length in enumerate(drawn.shape)]
    widest = drawn.shape.index(max(drawn.shape))
    next_to = place[:widest] + [(place[widest] + 1) % drawn.shape[widest]] + place[widest + 1:]
    return drawn.at[tuple(place)].set(low).at[tuple(next_to)].set(top_value)


def levels(key, dims, shards, low, largest):
    def one(dim, parts):
        draws = jax.random.uniform(jax.random.fold_in(jax.random.fold_in(key, 6), dim), (parts,), jnp.float32, low / len(shards), largest / len(shards))
        return jnp.repeat(jnp.exp(draws), dims[dim] // parts).reshape((-1,) + (1,) * (len(dims) - dim - 1))

    factor_of = one(*shards[0])
    for cut in shards[1:]:
        factor_of = factor_of * one(*cut)
    return factor_of


def noise(rng, dims, deviation, reach, shards=(), kind=jnp.bfloat16):
    entries = jax.random.normal(rng, dims, jnp.float32) * deviation
    if len(shards) > 0:
        entries = levels(rng, dims, shards, -0.22, 0.18) * entries
    return jnp.clip(entries, min=-reach, max=reach).astype(kind)


def setup_inputs(seed: int = 0) -> dict:
    key_of = jax.random.split(jax.random.key(seed), 7)
    return {
        "absorbed_query": draw_absorbed_query(jax.random.fold_in(key_of[6], 71), 0),
        "index_query": draw_index_query(jax.random.fold_in(key_of[6], 71), 0),
        "index_weight": noise(key_of[2], (ROWS, IDX_HEADS), 0.4, 2.0, ((0, 16), (1, 2))),
        "kv_cache": draw_kv_cache(jax.random.fold_in(key_of[6], 71), 0),
        "index_keys": draw_index_keys(jax.random.fold_in(key_of[6], 71), 0),
        "lengths": place_ends(jax.random.randint(key_of[5], (ROWS,), KEYS // 4, KEYS + 1), jax.random.fold_in(key_of[5], 1), KEYS // 4, KEYS).astype(jnp.int32),
    }


attention_scale = 192.0 ** -0.5


def reference(absorbed_query, index_query, index_weight, kv_cache, index_keys, lengths):
    key_index = jnp.arange(KEYS, dtype=jnp.int32)

    def one_row(packed):
        queries, idx_query, idx_weight, length = packed
        visible = key_index < length
        scores = jnp.dot(queries, kv_cache.T, preferred_element_type=jnp.float32) * attention_scale
        scores = jnp.where(visible[None, :], scores, -jnp.inf)
        att_max = jnp.max(scores, axis=1, keepdims=True)
        expo = jnp.exp(scores - att_max)
        summed = jnp.sum(expo / jnp.sum(expo, axis=1, keepdims=True), axis=0) / HEADS
        inner = jnp.dot(idx_query, index_keys.T, preferred_element_type=jnp.float32)
        logits = jnp.dot(idx_weight.astype(jnp.float32), jnp.maximum(inner, 0.0), precision=lax.Precision.HIGHEST) * IDX_DIM ** -0.5
        logits = jnp.where(visible, logits, -jnp.inf)
        idx_max = jnp.max(logits)
        idx_expo = jnp.exp(logits - idx_max)
        predicted = idx_expo / jnp.sum(idx_expo)
        return KEYS * summed, KEYS * (predicted - summed)

    target, gradient = lax.map(one_row, (absorbed_query, index_query, index_weight, lengths))
    return (target, gradient)
```

```python
import functools

import jax
import jax.numpy as jnp
from jax import lax
from jax.experimental import pallas as pl
from jax.experimental.pallas import tpu as pltpu
from jax.sharding import PartitionSpec as P

attention_scale = 192.0 ** (-0.5)
log2_e = 1.4426950408889634
far_below = -1e30
levels = 32767.0
lanes = 128
vmem_limit = 56 * 2**20


def sweep_kernel(
    row_count, head_count, idx_heads, latent, tile_keys, count, kept, ids, lengths, start, q_ref, kv_ref, ik_ref, *rest
):
    e_ref, top_ref, stat_ref, part_ref, s_a, s_b, m_a, m_b = rest[kept:]
    step = pl.program_id(0)
    queries = row_count * head_count
    keys = kv_ref.shape[0]
    idx_queries = row_count * idx_heads
    scale = attention_scale * log2_e
    first_row = ids[jnp.minimum(step, count - 1)] * row_count

    def scores(at, s_ref, m_ref, masked):
        y = lax.dot_general(
            q_ref[0, :queries, :],
            kv_ref[at : at + tile_keys, :],
            (((1,), (1,)), ((), ())),
            preferred_element_type=jnp.float32,
        )
        if masked:
            key = lax.broadcasted_iota(jnp.int32, (head_count, tile_keys), 1) + (start[0] + at)
            pieces = []
            for r in range(row_count):
                piece = y[r * head_count : (r + 1) * head_count]
                pieces.append(jnp.where(key < lengths[first_row + r], piece, -jnp.inf))
            y = jnp.concatenate(pieces, axis=0)
        s_ref[:, at : at + tile_keys] = y
        top = y[:, :lanes]
        for j in range(lanes, tile_keys, lanes):
            top = jnp.maximum(top, y[:, j : j + lanes])
        m_ref[...] = jnp.maximum(top, far_below if at == 0 else m_ref[...])

    def index_part(at):
        packed = q_ref[0, :, latent:]
        half = packed.shape[1]
        idx_query = jnp.concatenate([packed[:idx_queries], packed[idx_queries : 2 * idx_queries]], axis=1)
        weight = q_ref[0, queries : queries + 8, :lanes].astype(jnp.float32)[0:1]
        weight = jnp.transpose(jnp.broadcast_to(weight, (lanes, lanes)))
        inner = lax.dot_general(
            idx_query, ik_ref[at : at + tile_keys, :], (((1,), (1,)), ((), ())), preferred_element_type=jnp.float32
        )
        inner = jnp.maximum(inner, 0.0)
        for r in range(row_count):
            mine = slice(r * idx_heads, (r + 1) * idx_heads)
            for j in range(0, tile_keys, lanes):
                product = inner[mine, j : j + lanes] * weight[mine]
                part_ref[0, r : r + 1, at + j : at + j + lanes] = jnp.sum(product, axis=0, keepdims=True)

    def exponentials(at, s_ref, m_ref):
        for q in range(0, queries, 16):
            top = m_ref[q : q + 16, :]
            total = None
            for j in range(at, at + tile_keys, lanes):
                e = jnp.exp2((s_ref[q : q + 16, j : j + lanes] - top) * scale)
                total = e if total is None else total + e
                e_ref[0, q : q + 16, j : j + lanes] = jnp.round(e * levels).astype(jnp.int32).astype(jnp.int16)
            if at == 0:
                top_ref[0, q : q + 16, :] = total
            else:
                top_ref[0, q : q + 16, :] += total

    def finish(m_ref):
        top = jnp.transpose(m_ref[...])
        total = jnp.transpose(top_ref[0])
        largest = jnp.max(top, axis=0, keepdims=True)
        stat_ref[0, 0:1, :] = largest
        stat_ref[0, 1:2, :] = jnp.sum(total * jnp.exp2((top - largest) * scale), axis=0, keepdims=True)
        top_ref[0] = m_ref[...]

    def work(new, old, masked):
        for at in range(0, keys, tile_keys):
            if new is not None:
                scores(at, *new, masked)
                index_part(at)
            if old is not None:
                exponentials(at, *old)
        if old is not None:
            finish(old[1])

    shortest = lengths[first_row]
    for r in range(1, row_count):
        shortest = jnp.minimum(shortest, lengths[first_row + r])
    clear = shortest >= start[0] + keys
    odd = lax.rem(step, 2) == 1
    inside = jnp.logical_and(step > 0, step < count)
    a, b = (s_a, m_a), (s_b, m_b)
    pl.when(step == 0)(lambda: work(a, None, True))
    for parity, new, old in ((odd, b, a), (jnp.logical_not(odd), a, b)):
        here = jnp.logical_and(inside, parity)
        pl.when(jnp.logical_and(here, clear))(functools.partial(work, new, old, False))
        pl.when(jnp.logical_and(here, jnp.logical_not(clear)))(functools.partial(work, new, old, True))
    pl.when(step == count)(lambda: work(None, a if count % 2 == 1 else b, False))


def sweep(blocks, ids, kv, idx_keys, lengths, start, buffers, row_count, head_count, idx_heads, latent, total):
    count, block_rows, width = blocks.shape
    keys = kv.shape[0]
    queries = row_count * head_count
    outs = (
        jax.ShapeDtypeStruct((total, queries, keys), jnp.int16),
        jax.ShapeDtypeStruct((total, queries, lanes), jnp.float32),
        jax.ShapeDtypeStruct((total, 2, queries), jnp.float32),
        jax.ShapeDtypeStruct((total, row_count, keys), jnp.float32),
    )

    def now(step, ids, lengths, start):
        return (ids[jnp.minimum(step, count - 1)], 0, 0)

    def before(step, ids, lengths, start):
        return (ids[jnp.maximum(step - 1, 0)], 0, 0)

    kept = len(buffers)
    kernel = functools.partial(
        sweep_kernel, row_count, head_count, idx_heads, latent, min(512, keys), count, kept
    )
    return pl.pallas_call(
        kernel,
        out_shape=outs,
        grid_spec=pltpu.PrefetchScalarGridSpec(
            num_scalar_prefetch=3,
            grid=(count + 1,),
            in_specs=[
                pl.BlockSpec((1, block_rows, width), lambda step, *_: (jnp.minimum(step, count - 1), 0, 0)),
                pl.BlockSpec(kv.shape, lambda step, *_: (0, 0), pipeline_mode=pl.Buffered(1)),
                pl.BlockSpec(idx_keys.shape, lambda step, *_: (0, 0), pipeline_mode=pl.Buffered(1)),
            ]
            + [pl.BlockSpec(memory_space=pl.ANY)] * kept,
            out_specs=[
                pl.BlockSpec((1, queries, keys), before),
                pl.BlockSpec((1, queries, lanes), before),
                pl.BlockSpec((1, 2, queries), before),
                pl.BlockSpec((1, row_count, keys), now),
            ],
            scratch_shapes=[pltpu.VMEM((queries, keys), jnp.float32)] * 2
            + [pltpu.VMEM((queries, lanes), jnp.float32)] * 2,
        ),
        input_output_aliases={6 + k: k for k in range(kept)},
        compiler_params=pltpu.CompilerParams(vmem_limit_bytes=vmem_limit),
        cost_estimate=pl.CostEstimate(
            flops=2 * count * queries * keys * 1024,
            bytes_accessed=count * queries * keys * 2,
            transcendentals=count * queries * keys,
        ),
    )(ids, lengths, start, blocks, kv, idx_keys, *buffers)


def second_kernel(row_count, head_count, scale, whole, e_ref, top_ref, att_ref, logits_ref, idx_ref, t_ref, g_ref, c_ref):
    parts, groups, queries, keys = e_ref.shape

    @pl.when(pl.program_id(1) == 0)
    def _():
        for p in range(parts):
            for g in range(groups):
                largest = jnp.transpose(jnp.broadcast_to(att_ref[0, p, 0, g : g + 1, :], (lanes, queries)))
                factor = jnp.transpose(jnp.broadcast_to(att_ref[1, p, 0, g : g + 1, :], (lanes, queries)))
                c_ref[p, g] = jnp.exp2((top_ref[p, g] - largest) * scale) * factor

    for g in range(groups):
        for r in range(row_count):
            for j in range(0, keys, lanes):
                acc = None
                for p in range(parts):
                    for q in range(r * head_count, (r + 1) * head_count, 16):
                        term = e_ref[p, g, q : q + 16, j : j + lanes].astype(jnp.float32) * c_ref[p, g, q : q + 16, :]
                        acc = term if acc is None else acc + term
                row = g * row_count + r
                t_ref[row : row + 1, j : j + lanes] = jnp.sum(acc, axis=0, keepdims=True)
    predicted = jnp.exp(logits_ref[...] - idx_ref[0, :, 0:1]) * idx_ref[1, :, 0:1]
    g_ref[...] = predicted - t_ref[...]


def second(e, top, att, logits, idx, row_count, head_count, scale):
    parts, blocks, queries, keys = e.shape
    rows = blocks * row_count
    step_rows = min(8, rows)
    groups = step_rows // row_count
    tile_keys = min(1024, keys)
    shape = jax.ShapeDtypeStruct((rows, keys), jnp.float32)
    return pl.pallas_call(
        functools.partial(second_kernel, row_count, head_count, scale, keys),
        out_shape=(shape, shape),
        grid=(rows // step_rows, keys // tile_keys),
        in_specs=[
            pl.BlockSpec((parts, groups, queries, tile_keys), lambda i, u: (0, i, 0, u)),
            pl.BlockSpec((parts, groups, queries, lanes), lambda i, u: (0, i, 0, 0)),
            pl.BlockSpec((2, parts, 1, groups, queries), lambda i, u: (0, 0, i, 0, 0)),
            pl.BlockSpec((step_rows, tile_keys), lambda i, u: (i, u)),
            pl.BlockSpec((2, step_rows, lanes), lambda i, u: (0, i, 0)),
        ],
        out_specs=[pl.BlockSpec((step_rows, tile_keys), lambda i, u: (i, u))] * 2,
        scratch_shapes=[pltpu.VMEM((parts, groups, queries, lanes), jnp.float32)],
        compiler_params=pltpu.CompilerParams(vmem_limit_bytes=vmem_limit),
        cost_estimate=pl.CostEstimate(
            flops=2 * parts * blocks * queries * keys,
            bytes_accessed=parts * blocks * queries * keys * 2,
            transcendentals=rows * keys,
        ),
    )(e, top, att.reshape(2, parts, blocks // groups, groups, queries), logits, idx)


def swap(x, bit):
    size = lax.axis_size("ctx")
    return lax.ppermute(x, "ctx", [(i, i ^ bit) for i in range(size)])


def gathered(block):
    size = lax.axis_size("ctx")
    if size != 16:
        held, far, bit = block, [0], 1
        while bit < size:
            held = jnp.concatenate([held, swap(held, bit)])
            far = far + [k ^ bit for k in far]
            bit *= 2
        return [(held, far)]
    two = swap(block, 2)
    eight = swap(block, 8)
    near = jnp.concatenate([block, two])
    four = swap(near, 4)
    ten = swap(eight, 2)
    away = jnp.concatenate([eight, ten])
    twelve = swap(away, 4)
    groups = []
    for part, far in (
        (near, [0, 2]),
        (eight, [8]),
        (jnp.concatenate([four, ten]), [4, 6, 10]),
        (twelve, [12, 14]),
    ):
        both = jnp.concatenate([part, swap(part, 1)])
        groups.append((both, far + [k ^ 1 for k in far]))
    return groups


def body(absorbed_query, index_query, index_weight, kv_cache, index_keys, lengths):
    row_count, head_count, latent = absorbed_query.shape
    idx_heads, idx_width = index_query.shape[1:]
    ctx, head = lax.axis_size("ctx"), lax.axis_size("head")
    keys = kv_cache.shape[0]
    me, plane = lax.axis_index("ctx"), lax.axis_index("head")
    start = jnp.reshape(me * keys, (1,)).astype(jnp.int32)
    per = ctx // head
    own_rows = per * row_count
    own_lengths = lax.dynamic_slice_in_dim(lengths, plane * own_rows, own_rows)

    half = idx_width // 2
    idx_flat = index_query.reshape(row_count * idx_heads, idx_width)
    idx_packed = jnp.concatenate([idx_flat[:, :half], idx_flat[:, half:]])
    query = jnp.concatenate([absorbed_query.reshape(row_count * head_count, latent), idx_packed], axis=1)
    width = latent + half
    weight = index_weight.reshape(1, row_count * idx_heads)
    weight = jnp.pad(weight, ((0, 15), (0, width - weight.shape[1])))
    block = jnp.concatenate([query, weight])[None]

    moves = []
    for c in range(ctx):
        for h in range(head):
            moves.append((c * head + h, (h * per + c % per) * head + c // per))
    block = lax.ppermute(block, ("ctx", "head"), moves)

    kv = jnp.pad(kv_cache, ((0, 0), (0, half)))
    buffers = ()
    row_lengths = jnp.concatenate([own_lengths] * head)
    for blocks, far in gathered(block):
        ids = jnp.bitwise_xor(me, jnp.array(far, jnp.int32)).astype(jnp.int32)
        buffers = sweep(
            blocks, ids, kv, index_keys, row_lengths, start, buffers, row_count, head_count, idx_heads, latent, ctx
        )
    e, top, stat, part = buffers
    queries = row_count * head_count

    key = start[0] + jnp.arange(keys, dtype=jnp.int32)
    logits = jnp.sum(part.reshape(head, own_rows, keys), axis=0) * idx_width ** (-0.5)
    logits = jnp.where(key[None, :] < own_lengths[:, None], logits, -jnp.inf)
    idx_max = jnp.maximum(jnp.max(logits, axis=-1), far_below)
    idx_total = jnp.sum(jnp.exp(logits - idx_max[:, None]), axis=-1)

    largest = jnp.concatenate([stat[:, 0, :].reshape(-1) * attention_scale, idx_max])
    total = jnp.concatenate([stat[:, 1, :].reshape(-1), idx_total])
    state = jnp.stack([largest, total])
    bit = 1
    while bit < ctx:
        other = swap(state, bit)
        top_two = jnp.maximum(state[0], other[0])
        merged = state[1] * jnp.exp(state[0] - top_two) + other[1] * jnp.exp(other[0] - top_two)
        state = jnp.stack([top_two, merged])
        bit *= 2
    whole = float(keys * ctx)
    factor = whole / (levels * head * head_count)
    att = jnp.stack([state[0, : ctx * queries] * (1.0 / attention_scale), factor / state[1, : ctx * queries]])
    att = att.reshape(2, head, per, queries)
    idx = jnp.stack([state[0, ctx * queries :], whole / state[1, ctx * queries :]])
    idx = jnp.broadcast_to(idx[:, :, None], idx.shape + (lanes,))
    shape = (head, per, queries)
    return second(
        e.reshape(shape + (keys,)),
        top.reshape(shape + (lanes,)),
        att,
        logits,
        idx,
        row_count,
        head_count,
        attention_scale * log2_e,
    )


def solution(mesh):
    return jax.shard_map(
        body,
        mesh=mesh,
        in_specs=(
            P("ctx", "head", None),
            P("ctx", "head", None),
            P("ctx", "head"),
            P("ctx", None),
            P("ctx", None),
            P(),
        ),
        out_specs=(P("head", "ctx"), P("head", "ctx")),
        check_vma=False,
    )
```

```python
import functools

import jax
import jax.numpy as jnp
from jax import lax
from jax.experimental import pallas as pl
from jax.experimental.pallas import tpu as pltpu
from jax.sharding import PartitionSpec as P

attention_scale = 192.0 ** (-0.5)
log2_e = 1.4426950408889634
far_below = -1e30
levels = 32767.0
lanes = 128
vmem_limit = 20 * 2**20
second_vmem = 57 * 2**20


def sweep_kernel(row_count, head_count, idx_heads, latent, spans, sizes, resident, info, kv_ref, ik_ref, *rest):
    sources, rest = rest[: len(sizes)], rest[len(sizes) :]
    e_ref, e_last, top_ref, top_last, stat_ref, part_ref, done_ref, *rest = rest
    s_a, s_b, m_a, m_b, run_m, run_t, turn_m, turn_t, q_slots, q_sems = rest
    count = sum(sizes)
    step = pl.program_id(0)
    queries = row_count * head_count
    keys = kv_ref.shape[1]
    span = keys // spans
    idx_queries = row_count * idx_heads
    scale = attention_scale * log2_e
    start = info[0]
    place = info[1 + jnp.minimum(step, count - 1)]
    before = info[1 + jnp.maximum(step - 1, 0)]
    first_row = 1 + count + place * row_count
    pairs = ((s_a, m_a), (s_b, m_b))

    def scores(u, masked):
        s_ref, m_ref = pairs[u % 2]
        for at in range(0, span, min(512, span)):
            size = min(512, span)
            y = jnp.dot(
                q_ref[:queries, :latent],
                kv_ref[:, u * span + at : u * span + at + size],
                preferred_element_type=jnp.float32,
            )
            if masked:
                key = lax.broadcasted_iota(jnp.int32, (head_count, size), 1) + (start + u * span + at)
                pieces = []
                for r in range(row_count):
                    piece = y[r * head_count : (r + 1) * head_count]
                    pieces.append(jnp.where(key < info[first_row + r], piece, -jnp.inf))
                y = jnp.concatenate(pieces, axis=0)
            s_ref[:, at : at + size] = y
            top = y[:, :lanes]
            for j in range(lanes, size, lanes):
                top = jnp.maximum(top, y[:, j : j + lanes])
            m_ref[...] = jnp.maximum(top, far_below if at == 0 else m_ref[...])

    def index_part(u):
        packed = q_ref[: 2 * idx_queries, latent:]
        idx_query = jnp.concatenate([packed[:idx_queries], packed[idx_queries:]], axis=1)
        weight = q_ref[queries : queries + 8, :lanes].astype(jnp.float32)[0:1]
        weight = jnp.transpose(jnp.broadcast_to(weight, (lanes, lanes)))[:idx_queries]
        for at in range(u * span, (u + 1) * span, min(256, span)):
            size = min(256, span)
            inner = lax.dot_general(
                idx_query, ik_ref[at : at + size, :], (((1,), (1,)), ((), ())), preferred_element_type=jnp.float32
            )
            for j in range(0, size, lanes):
                product = jnp.maximum(inner[:, j : j + lanes], 0.0) * weight
                product = jnp.sum(product.reshape(row_count, idx_heads, lanes), axis=1)
                part_ref[0, :, at + j : at + j + lanes] = product

    def exponentials(u, where):
        s_ref, m_ref = pairs[u % 2]
        if resident:
            out, top_out, shift, column = e_ref.at[where], top_ref.at[where], u * span, u * lanes
        elif u < spans - 1:
            out, top_out, shift, column = e_ref.at[0], top_ref.at[0], u * span, u * lanes
        else:
            out, top_out, shift, column = e_last.at[0], top_last.at[0], 0, 0
        for q in range(0, queries, 16):
            top = m_ref[q : q + 16, :]
            total = None
            for j in range(0, span, lanes):
                e = jnp.exp2((s_ref[q : q + 16, j : j + lanes] - top) * scale)
                total = e if total is None else total + e
                out[q : q + 16, shift + j : shift + j + lanes] = jnp.round(e * levels).astype(jnp.int32).astype(jnp.int16)
            top_out[q : q + 16, column : column + lanes] = top
            if u == 0:
                run_m[q : q + 16, :] = top
                run_t[q : q + 16, :] = total
            else:
                held = run_m[q : q + 16, :]
                larger = jnp.maximum(held, top)
                run_m[q : q + 16, :] = larger
                run_t[q : q + 16, :] = run_t[q : q + 16, :] * jnp.exp2((held - larger) * scale) + total * jnp.exp2(
                    (top - larger) * scale
                )

    def turn():
        turn_m[...] = jnp.transpose(run_m[...])
        turn_t[...] = jnp.transpose(run_t[...])

    def finish():
        top = turn_m[...]
        largest = jnp.max(top, axis=0, keepdims=True)
        stat_ref[0, 0:1, :] = largest
        stat_ref[0, 1:2, :] = jnp.sum(turn_t[...] * jnp.exp2((top - largest) * scale), axis=0, keepdims=True)

    def work(masked):
        scores(0, masked)
        index_part(0)
        exponentials(spans - 1, before)
        for u in range(1, spans):
            scores(u, masked)
            if u == 1:
                turn()
            if u == 2:
                finish()
            index_part(u)
            exponentials(u - 1, place)

    def last():
        exponentials(spans - 1, before)
        turn()
        finish()
        done_ref[0] = 0

    shortest = info[first_row]
    for r in range(1, row_count):
        shortest = jnp.minimum(shortest, info[first_row + r])
    clear = shortest >= start + keys
    inside = step < count
    slot = lax.rem(step, 2)
    q_ref = q_slots.at[slot]

    def query_copy(tile, act):
        passed = 0
        for source, size in zip(sources, sizes):

            @pl.when(jnp.logical_and(tile >= passed, tile < passed + size))
            def _(source=source, passed=passed):
                into = lax.rem(tile, 2)
                act(pltpu.make_async_copy(source.at[tile - passed], q_slots.at[into], q_sems.at[into]))

            passed += size

    pl.when(step == 0)(lambda: query_copy(step, lambda copy: copy.start()))
    query_copy(step, lambda copy: copy.wait())
    query_copy(step + 1, lambda copy: copy.start())
    pl.when(jnp.logical_and(inside, clear))(lambda: work(False))
    pl.when(jnp.logical_and(inside, jnp.logical_not(clear)))(lambda: work(True))
    pl.when(step == count)(last)


def sweep(blocks, info, kv, idx_keys, resident, row_count, head_count, idx_heads, latent):
    sizes = [a.shape[0] for a in blocks]
    count = sum(sizes)
    block_rows, width = blocks[0].shape[1:]
    keys = kv.shape[1]
    queries = row_count * head_count
    spans = 4
    span = keys // spans
    kept, tops = (span, lanes) if not resident else (0, 0)
    space = pltpu.VMEM if resident else pltpu.HBM
    outs = (
        space((count, queries, keys - kept), jnp.int16),
        pltpu.HBM((count, queries, span) if kept else (1, 16, lanes), jnp.int16),
        space((count, queries, spans * lanes - tops), jnp.float32),
        pltpu.HBM((count, queries, lanes) if kept else (1, 8, lanes), jnp.float32),
        pltpu.HBM((count, 2, queries), jnp.float32),
        pltpu.HBM((count, row_count, keys), jnp.float32),
        jax.ShapeDtypeStruct((1,), jnp.int32),
    )

    def now(step, info):
        return (info[1 + jnp.minimum(step, count - 1)], 0, 0)

    def before(step, info):
        return (info[1 + jnp.maximum(step - 1, 0)], 0, 0)

    kernel = functools.partial(sweep_kernel, row_count, head_count, idx_heads, latent, spans, sizes, resident)
    whole = pl.BlockSpec(memory_space=pltpu.VMEM)
    unused = pl.BlockSpec(memory_space=pl.ANY)
    return pl.pallas_call(
        kernel,
        out_shape=outs,
        grid_spec=pltpu.PrefetchScalarGridSpec(
            num_scalar_prefetch=1,
            grid=(count + 1,),
            in_specs=[whole, whole] + [pl.BlockSpec(memory_space=pltpu.HBM)] * len(blocks),
            out_specs=[
                whole if resident else pl.BlockSpec((1, queries, keys - span), now),
                unused if resident else pl.BlockSpec((1, queries, span), before),
                whole if resident else pl.BlockSpec((1, queries, (spans - 1) * lanes), now),
                unused if resident else pl.BlockSpec((1, queries, lanes), before),
                pl.BlockSpec((1, 2, queries), before),
                pl.BlockSpec((1, row_count, keys), now),
                pl.BlockSpec(memory_space=pltpu.SMEM),
            ],
            scratch_shapes=[pltpu.VMEM((queries, span), jnp.float32)] * 2
            + [pltpu.VMEM((queries, lanes), jnp.float32)] * 4
            + [pltpu.VMEM((lanes, queries), jnp.float32)] * 2
            + [pltpu.VMEM((2, block_rows, width), jnp.bfloat16), pltpu.SemaphoreType.DMA((2,))],
        ),
        compiler_params=pltpu.CompilerParams(vmem_limit_bytes=vmem_limit),
        cost_estimate=pl.CostEstimate(
            flops=2 * count * queries * keys * 1024,
            bytes_accessed=count * queries * keys * 2,
            transcendentals=count * queries * keys,
        ),
    )(info, kv, idx_keys, *blocks)


def second_kernel(row_count, head_count, scale, spans, per, layout, *refs):
    sets = []
    for parts, resident in layout:
        sets.append((parts, resident, refs[: 2 if resident else 4]))
        refs = refs[2 if resident else 4 :]
    att_ref, logits_ref, idx_ref, t_ref, g_ref, c_ref, turn_ref, sum_ref = refs
    queries = c_ref.shape[2]
    keys = t_ref.shape[1]
    span = keys // spans
    groups = t_ref.shape[0] // row_count
    group = pl.program_id(1)
    first = pl.program_id(0) * groups + group

    members = []
    for parts, resident, arrays in sets:
        for p in range(parts):
            index = len(members)
            if resident:

                def take(u, p=p, arrays=arrays):
                    e, top = arrays
                    return e.at[p * per + first], u * span, top[p * per + first, :, u * lanes : (u + 1) * lanes]

            else:

                def take(u, p=p, arrays=arrays):
                    e, e_last, top, top_last = arrays
                    if u < spans - 1:
                        return e.at[p, 0], u * span, top[p, 0, :, u * lanes : (u + 1) * lanes]
                    return e_last.at[p, 0], 0, top_last[p, 0]

            members.append((index * per + first, take))

    for p, (place, _) in enumerate(members):
        turn_ref[0, p] = jnp.transpose(jnp.broadcast_to(att_ref[0, place], (lanes, queries)))
        turn_ref[1, p] = jnp.transpose(jnp.broadcast_to(att_ref[1, place], (lanes, queries)))

    def factors(u):
        for p, (_, take) in enumerate(members):
            c_ref[u, p] = jnp.exp2((take(u)[2] - turn_ref[0, p]) * scale) * turn_ref[1, p]

    factors(0)
    for u in range(spans):
        if u + 1 < spans:
            factors(u + 1)
        for r in range(row_count):
            acc = [None] * (span // lanes)
            for p, (_, take) in enumerate(members):
                source, shift, _ = take(u)
                for q in range(r * head_count, (r + 1) * head_count, 16):
                    c = c_ref[u, p, q : q + 16, :]
                    for k in range(len(acc)):
                        at = shift + k * lanes
                        term = source[q : q + 16, at : at + lanes].astype(jnp.float32) * c
                        term = term[:8] + term[8:]
                        acc[k] = term if acc[k] is None else acc[k] + term
            for k in range(len(acc)):
                at = u * span + k * lanes
                sum_ref[group, r : r + 1, at : at + lanes] = jnp.sum(acc[k], axis=0, keepdims=True)

    @pl.when(group == groups - 1)
    def _():
        target = jnp.concatenate([sum_ref[g] for g in range(groups)], axis=0)
        predicted = jnp.exp(logits_ref[...] - idx_ref[0, :, 0:1]) * idx_ref[1, :, 0:1]
        t_ref[...] = target
        g_ref[...] = predicted - target


def second(sets, att, logits, idx, row_count, head_count, scale):
    rows, keys = logits.shape
    queries = row_count * head_count
    spans = 4
    span = keys // spans
    per = rows // row_count
    step_rows = min(8, rows)
    groups = step_rows // row_count
    shape = jax.ShapeDtypeStruct((rows, keys), jnp.float32)
    whole = pl.BlockSpec(memory_space=pltpu.VMEM)

    def mine(i, g):
        return (0, i * groups + g, 0, 0)

    operands, specs, total = [], [], 0
    for (e, e_last, top, top_last), parts, resident in sets:
        total += parts
        if resident:
            operands += [e, top]
            specs += [whole, whole]
        else:
            for a in (e, e_last, top, top_last):
                operands.append(a.reshape((parts, per) + a.shape[1:]))
                specs.append(pl.BlockSpec((parts, 1) + a.shape[1:], mine))
    return pl.pallas_call(
        functools.partial(
            second_kernel, row_count, head_count, scale, spans, per, [(parts, resident) for _, parts, resident in sets]
        ),
        out_shape=(shape, shape),
        grid=(rows // step_rows, groups),
        in_specs=specs
        + [
            pl.BlockSpec((2, total * per, 1, queries), lambda i, g: (0, 0, 0, 0)),
            pl.BlockSpec((step_rows, keys), lambda i, g: (i, 0)),
            pl.BlockSpec((2, step_rows, lanes), lambda i, g: (0, i, 0)),
        ],
        out_specs=[pl.BlockSpec((step_rows, keys), lambda i, g: (i, 0))] * 2,
        scratch_shapes=[
            pltpu.VMEM((spans, total, queries, lanes), jnp.float32),
            pltpu.VMEM((2, total, queries, lanes), jnp.float32),
            pltpu.VMEM((groups, row_count, keys), jnp.float32),
        ],
        compiler_params=pltpu.CompilerParams(vmem_limit_bytes=second_vmem),
        cost_estimate=pl.CostEstimate(
            flops=2 * total * per * queries * keys,
            bytes_accessed=total * per * queries * keys * 2,
            transcendentals=rows * keys,
        ),
    )(*operands, att[:, :, None, :], logits, idx)


def logits_kernel(row_count, scale, lengths, start, *refs):
    *part_refs, logits_ref, idx_ref = refs
    rows, keys = logits_ref.shape
    per = rows // row_count
    key = lax.broadcasted_iota(jnp.int32, (row_count, keys), 1) + start[0]
    row = lax.broadcasted_iota(jnp.int32, (row_count, keys), 0)
    for i in range(per):
        value = None
        for part in part_refs:
            for p in range(i, part.shape[0], per):
                value = part[p] if value is None else value + part[p]
        length = jnp.full((row_count, keys), lengths[i * row_count], jnp.int32)
        for r in range(1, row_count):
            length = jnp.where(row == r, lengths[i * row_count + r], length)
        value = jnp.where(key < length, value * scale, -jnp.inf)
        logits_ref[i * row_count : (i + 1) * row_count, :] = value
        largest = jnp.maximum(jnp.max(value, axis=1, keepdims=True), far_below)
        rest = jnp.sum(jnp.exp(value - largest), axis=1, keepdims=True)
        idx_ref[0, i * row_count : (i + 1) * row_count, :] = jnp.broadcast_to(largest, (row_count, lanes))
        idx_ref[1, i * row_count : (i + 1) * row_count, :] = jnp.broadcast_to(rest, (row_count, lanes))


def index_logits(parts, lengths, start, scale):
    row_count, keys = parts[0].shape[1:]
    rows = lengths.shape[0]
    scalars = pl.BlockSpec(memory_space=pltpu.SMEM)
    return pl.pallas_call(
        functools.partial(logits_kernel, row_count, scale),
        out_shape=(
            jax.ShapeDtypeStruct((rows, keys), jnp.float32),
            jax.ShapeDtypeStruct((2, rows, lanes), jnp.float32),
        ),
        in_specs=[scalars, scalars] + [pl.BlockSpec(memory_space=pltpu.VMEM)] * len(parts),
        compiler_params=pltpu.CompilerParams(vmem_limit_bytes=32 * 2**20),
    )(lengths, start, *parts)


def swap(x, bit):
    size = lax.axis_size("ctx")
    return lax.ppermute(x, "ctx", [(i, i ^ bit) for i in range(size)])


def across(x):
    return lax.ppermute(x, "head", [(0, 1), (1, 0)])


def bring_and_sweep(block, sweep_blocks):
    ctx, head = lax.axis_size("ctx"), lax.axis_size("head")
    me, plane = lax.axis_index("ctx"), lax.axis_index("head")
    per = ctx // head
    if ctx != 16 or head != 2:
        moves = []
        for c in range(ctx):
            for h in range(head):
                moves.append((c * head + h, (h * per + c % per) * head + c // per))
        held, far, bit = lax.ppermute(block, ("ctx", "head"), moves), [0], 1
        while bit < ctx:
            held = jnp.concatenate([held, swap(held, bit)])
            far = far + [k ^ bit for k in far]
            bit *= 2
        return [sweep_blocks([held], [jnp.bitwise_xor(me, k) for k in far], False, head)]
    half = ctx // 2
    home = me // half == plane
    mine = lax.rem(me, half)

    def place(distance):
        return mine ^ distance

    away = swap(block, half)
    beside = across(block)
    away_beside = across(away)
    one = jnp.where(home, block, away)
    one_x, one_z = swap(one, 2), swap(one, 4)
    two = jnp.where(home, beside, away_beside)
    two_x, two_z = swap(two, 2), swap(two, 4)
    one_zx = swap(one_z, 2)
    two_xz = swap(two_x, 4)
    swept = []
    for part in ([one, one_x, one_z, one_zx], [two, two_x, two_z, two_xz]):
        blocks = part + [swap(a, 1) for a in part]
        swept.append(sweep_blocks(blocks, [place(k) for k in (0, 2, 4, 6, 1, 3, 5, 7)], False, 1))
    return swept


def body(absorbed_query, index_query, index_weight, kv_cache, index_keys, lengths):
    row_count, head_count, latent = absorbed_query.shape
    idx_heads, idx_width = index_query.shape[1:]
    ctx, head = lax.axis_size("ctx"), lax.axis_size("head")
    keys = kv_cache.shape[0]
    me, plane = lax.axis_index("ctx"), lax.axis_index("head")
    start = jnp.reshape(me * keys, (1,)).astype(jnp.int32)
    per = ctx // head
    own_rows = per * row_count
    own_lengths = lax.dynamic_slice_in_dim(lengths, plane * own_rows, own_rows)

    half = idx_width // 2
    idx_flat = index_query.reshape(row_count * idx_heads, idx_width)
    idx_packed = jnp.concatenate([idx_flat[:, :half], idx_flat[:, half:]])
    query = jnp.concatenate([absorbed_query.reshape(row_count * head_count, latent), idx_packed], axis=1)
    width = latent + half
    weight = index_weight.reshape(1, row_count * idx_heads)
    weight = jnp.pad(weight, ((0, 15), (0, width - weight.shape[1])))
    block = jnp.concatenate([query, weight])[None]

    kv = kv_cache.T

    def sweep_blocks(blocks, places, resident, parts):
        info = jnp.concatenate([start, jnp.stack(places).astype(jnp.int32)] + [own_lengths] * parts)
        return sweep(blocks, info, kv, index_keys, resident, row_count, head_count, idx_heads, latent)

    swept = bring_and_sweep(block, sweep_blocks)
    sets = []
    for arrays in swept:
        parts = arrays[4].shape[0] // per
        sets.append((arrays[:4], parts, arrays[0].shape[-1] == keys))
    stat = jnp.concatenate([arrays[4] for arrays in swept])
    queries = row_count * head_count

    logits, idx = index_logits([arrays[5] for arrays in swept], own_lengths, start, idx_width ** (-0.5))
    idx_max, idx_total = idx[0, :, 0], idx[1, :, 0]

    largest = jnp.concatenate([stat[:, 0, :].reshape(-1) * attention_scale, idx_max])
    total = jnp.concatenate([stat[:, 1, :].reshape(-1), idx_total])
    state = jnp.stack([largest, total])
    bit = 1
    while bit < ctx:
        other = swap(state, bit)
        top_two = jnp.maximum(state[0], other[0])
        merged = state[1] * jnp.exp(state[0] - top_two) + other[1] * jnp.exp(other[0] - top_two)
        state = jnp.stack([top_two, merged])
        bit *= 2
    whole = float(keys * ctx)
    factor = whole / (levels * head * head_count)
    att = jnp.stack([state[0, : ctx * queries] * (1.0 / attention_scale), factor / state[1, : ctx * queries]])
    att = att.reshape(2, ctx, queries)
    idx = jnp.stack([state[0, ctx * queries :], whole / state[1, ctx * queries :]])
    idx = jnp.broadcast_to(idx[:, :, None], idx.shape + (lanes,))
    return second(sets, att, logits, idx, row_count, head_count, attention_scale * log2_e)


def solution(mesh):
    return jax.shard_map(
        body,
        mesh=mesh,
        in_specs=(
            P("ctx", "head", None),
            P("ctx", "head", None),
            P("ctx", "head"),
            P("ctx", None),
            P("ctx", None),
            P(),
        ),
        out_specs=(P("head", "ctx"), P("head", "ctx")),
        check_vma=False,
    )
```

```python
import functools

import jax
import jax.numpy as jnp
from jax import lax
from jax.experimental import pallas as pl
from jax.experimental.pallas import tpu as pltpu
from jax.sharding import PartitionSpec as P

attention_scale = 192.0 ** (-0.5)
log2_e = 1.4426950408889634
far_below = -1e30
levels = 32767.0
lanes = 128
span_count = 4
lag = 2
vmem_limit = 32 * 2**20
second_vmem = 57 * 2**20


def sweep_kernel(row_count, head_count, idx_heads, latent, spans, pack, sizes, info, kv_ref, ik_ref, *rest):
    sources, rest = rest[: len(sizes)], rest[len(sizes) :]
    e_hbm, top_hbm, stat_ref, part_ref, *rest = rest
    e_slots, top_slots, s_all, m_all, run_m, run_t, turn_m, turn_t, iq_ref, w_ref, q_slots, e_sems, top_sems, q_sems = rest
    count = sum(sizes)
    queries = row_count * head_count
    keys = kv_ref.shape[1]
    span = keys // spans
    idx_queries = row_count * idx_heads
    scale = attention_scale * log2_e
    start = info[0]

    def query_copy(tile, act):
        passed = 0
        for source, size in zip(sources, sizes):

            @pl.when(jnp.logical_and(tile >= passed, tile < passed + size))
            def _(source=source, passed=passed):
                into = lax.rem(tile, 2 * pack)
                act(pltpu.make_async_copy(source.at[tile - passed], q_slots.at[into], q_sems.at[into]))

            passed += size

    def result_copies(tile, act):
        slot, place = lax.rem(tile, 3 * pack), info[1 + tile]
        act(pltpu.make_async_copy(e_slots.at[slot], e_hbm.at[place], e_sems.at[slot]))
        act(pltpu.make_async_copy(top_slots.at[slot], top_hbm.at[place], top_sems.at[slot]))

    def begin(copy):
        copy.start()

    def await_end(copy):
        copy.wait()

    def scores(u, q_ref, first_row, masked):
        s_ref, m_ref = s_all.at[u], m_all.at[u]
        for at in range(0, span, min(512, span)):
            size = min(512, span)
            y = jnp.dot(
                q_ref[:queries, :latent],
                kv_ref[:, u * span + at : u * span + at + size],
                preferred_element_type=jnp.float32,
            )
            if masked:
                key = lax.broadcasted_iota(jnp.int32, (head_count, size), 1) + (start + u * span + at)
                pieces = []
                for r in range(row_count):
                    piece = y[r * head_count : (r + 1) * head_count]
                    pieces.append(jnp.where(key < info[first_row + r], piece, -jnp.inf))
                y = jnp.concatenate(pieces, axis=0)
            s_ref[:, at : at + size] = y
            top = y[:, :lanes]
            for j in range(lanes, size, lanes):
                top = jnp.maximum(top, y[:, j : j + lanes])
            m_ref[...] = jnp.maximum(top, far_below if at == 0 else m_ref[...])

    def index_part(u, q_ref, place):
        if u == 0:
            packed = q_ref[: 2 * idx_queries, latent:]
            iq_ref[...] = jnp.concatenate([packed[:idx_queries], packed[idx_queries:]], axis=1)
            weight = q_ref[queries : queries + 8, :lanes].astype(jnp.float32)[0:1]
            w_ref[...] = jnp.transpose(jnp.broadcast_to(weight, (lanes, lanes)))[:idx_queries]
        for at in range(u * span, (u + 1) * span, min(256, span)):
            size = min(256, span)
            inner = lax.dot_general(
                iq_ref[...], ik_ref[at : at + size, :], (((1,), (1,)), ((), ())), preferred_element_type=jnp.float32
            )
            for j in range(0, size, lanes):
                product = jnp.maximum(inner[:, j : j + lanes], 0.0) * w_ref[...]
                product = jnp.sum(product.reshape(row_count, idx_heads, lanes), axis=1)
                part_ref[place, :, at + j : at + j + lanes] = product

    def exponentials(u, slot):
        s_ref, m_ref = s_all.at[u], m_all.at[u]
        out, top_out = e_slots.at[slot], top_slots.at[slot]
        for q in range(0, queries, 16):
            top = m_ref[q : q + 16, :]
            total = None
            for j in range(0, span, lanes):
                e = jnp.exp2((s_ref[q : q + 16, j : j + lanes] - top) * scale)
                total = e if total is None else total + e
                out[q : q + 16, u * span + j : u * span + j + lanes] = jnp.round(e * levels).astype(jnp.int32).astype(jnp.int16)
            top_out[q : q + 16, u * lanes : (u + 1) * lanes] = top
            if u == 0:
                run_m[q : q + 16, :] = top
                run_t[q : q + 16, :] = total
            else:
                held = run_m[q : q + 16, :]
                larger = jnp.maximum(held, top)
                run_m[q : q + 16, :] = larger
                run_t[q : q + 16, :] = run_t[q : q + 16, :] * jnp.exp2((held - larger) * scale) + total * jnp.exp2(
                    (top - larger) * scale
                )

    def turn():
        turn_m[...] = jnp.transpose(run_m[...])
        turn_t[...] = jnp.transpose(run_t[...])

    def finish(place):
        top = turn_m[...]
        largest = jnp.max(top, axis=0, keepdims=True)
        stat_ref[place, 0:1, :] = largest
        stat_ref[place, 1:2, :] = jnp.sum(turn_t[...] * jnp.exp2((top - largest) * scale), axis=0, keepdims=True)

    def guarded(tile, action):
        pl.when(jnp.logical_and(tile >= 0, tile < count))(action)

    def boundary(i):
        for k in range(pack):
            old, done = pack * (i - 2) - 1 + k, pack * (i - 1) - 1 + k
            guarded(old, functools.partial(result_copies, old, await_end))
            guarded(done, functools.partial(result_copies, done, begin))

    def step(i, _):
        tiles = [i * pack + k for k in range(pack)]
        rows = [1 + count + info[1 + tile] * row_count for tile in tiles]
        shortest = info[rows[0]]
        for first_row in rows:
            for r in range(row_count):
                shortest = jnp.minimum(shortest, info[first_row + r])
        clear = shortest >= start + keys
        for tile in tiles:
            query_copy(tile, await_end)
        for tile in tiles:
            query_copy(tile + pack, begin)
        boundary(i)

        def work(masked):
            for tile, first_row in zip(tiles, rows):
                slot = lax.rem(tile, 3 * pack)
                other = lax.rem(tile + 3 * pack - 1, 3 * pack)
                q_ref = q_slots.at[lax.rem(tile, 2 * pack)]
                place = info[1 + tile]
                before = info[1 + jnp.maximum(tile - 1, 0)]
                for u in range(spans):
                    scores(u, q_ref, first_row, masked)
                    if u == lag:
                        turn()
                    index_part(u, q_ref, place)
                    exponentials((u - lag) % spans, other if u < lag else slot)
                    if u == min(lag + 1, spans - 1):
                        finish(before)

        pl.when(clear)(lambda: work(False))
        pl.when(jnp.logical_not(clear))(lambda: work(True))
        return 0

    steps = count // pack
    for tile in range(pack):
        query_copy(tile, begin)
    lax.fori_loop(0, steps, step, 0)
    boundary(steps)
    for u in range(spans - lag, spans):
        exponentials(u, (count - 1) % (3 * pack))
    result_copies(count - 1, begin)
    turn()
    finish(info[count])
    for tile in range(max(0, count - 1 - pack), count):
        result_copies(tile, await_end)


def sweep(blocks, info, kv, idx_keys, row_count, head_count, idx_heads, latent):
    sizes = [a.shape[0] for a in blocks]
    count = sum(sizes)
    block_rows, width = blocks[0].shape[1:]
    keys = kv.shape[1]
    queries = row_count * head_count
    spans = span_count
    span = keys // spans
    pack = 1
    kernel = functools.partial(sweep_kernel, row_count, head_count, idx_heads, latent, spans, pack, sizes)
    whole = pl.BlockSpec(memory_space=pltpu.VMEM)
    far = pl.BlockSpec(memory_space=pltpu.HBM)
    return pl.pallas_call(
        kernel,
        out_shape=(
            pltpu.HBM((count, queries, keys), jnp.int16),
            pltpu.HBM((count, queries, spans * lanes), jnp.float32),
            jax.ShapeDtypeStruct((count, 2, queries), jnp.float32),
            jax.ShapeDtypeStruct((count, row_count, keys), jnp.float32),
        ),
        in_specs=[pl.BlockSpec(memory_space=pltpu.SMEM), whole, whole] + [far] * len(blocks),
        out_specs=[far, far, whole, whole],
        scratch_shapes=[
            pltpu.VMEM((3 * pack, queries, keys), jnp.int16),
            pltpu.VMEM((3 * pack, queries, spans * lanes), jnp.float32),
        ]
        + [pltpu.VMEM((spans, queries, span), jnp.float32), pltpu.VMEM((spans, queries, lanes), jnp.float32)]
        + [pltpu.VMEM((queries, lanes), jnp.float32)] * 2
        + [pltpu.VMEM((lanes, queries), jnp.float32)] * 2
        + [pltpu.VMEM((row_count * idx_heads, idx_keys.shape[1]), jnp.bfloat16)]
        + [pltpu.VMEM((row_count * idx_heads, lanes), jnp.float32)]
        + [pltpu.VMEM((2 * pack, block_rows, width), jnp.bfloat16)]
        + [pltpu.SemaphoreType.DMA((3 * pack,))] * 2
        + [pltpu.SemaphoreType.DMA((2 * pack,))],
        compiler_params=pltpu.CompilerParams(vmem_limit_bytes=vmem_limit),
        cost_estimate=pl.CostEstimate(
            flops=2 * count * queries * keys * 1024,
            bytes_accessed=count * queries * keys * 2,
            transcendentals=count * queries * keys,
        ),
    )(info, kv, idx_keys, *blocks)


def second_kernel(row_count, head_count, scale, spans, per, layout, *refs):
    arrays, refs = refs[: 2 * len(layout)], refs[2 * len(layout) :]
    att_ref, logits_ref, idx_ref, t_ref, g_ref, c_ref, turn_ref, sum_ref = refs
    queries = c_ref.shape[2]
    keys = t_ref.shape[1]
    span = keys // spans
    groups = t_ref.shape[0] // row_count
    group = pl.program_id(1)
    first = pl.program_id(0) * groups + group

    members = []
    for k, parts in enumerate(layout):
        for p in range(parts):
            members.append((len(members) * per + first, arrays[2 * k].at[p, 0], arrays[2 * k + 1].at[p, 0]))

    for p, (place, _, _) in enumerate(members):
        turn_ref[0, p] = jnp.transpose(jnp.broadcast_to(att_ref[0, place], (lanes, queries)))
        turn_ref[1, p] = jnp.transpose(jnp.broadcast_to(att_ref[1, place], (lanes, queries)))

    def factors(u):
        for p, (_, _, top) in enumerate(members):
            top_u = top[:, u * lanes : (u + 1) * lanes]
            c_ref[u, p] = jnp.exp2((top_u - turn_ref[0, p]) * scale) * turn_ref[1, p]

    factors(0)
    for u in range(spans):
        if u + 1 < spans:
            factors(u + 1)
        for r in range(row_count):
            acc = [None] * (span // lanes)
            for p, (_, source, _) in enumerate(members):
                for q in range(r * head_count, (r + 1) * head_count, 16):
                    c = c_ref[u, p, q : q + 16, :]
                    for k in range(len(acc)):
                        at = u * span + k * lanes
                        term = source[q : q + 16, at : at + lanes].astype(jnp.float32) * c
                        term = term[:8] + term[8:]
                        acc[k] = term if acc[k] is None else acc[k] + term
            for k in range(len(acc)):
                at = u * span + k * lanes
                sum_ref[group, r : r + 1, at : at + lanes] = jnp.sum(acc[k], axis=0, keepdims=True)

    @pl.when(group == groups - 1)
    def _():
        target = jnp.concatenate([sum_ref[g] for g in range(groups)], axis=0)
        predicted = jnp.exp(logits_ref[...] - idx_ref[0, :, 0:1]) * idx_ref[1, :, 0:1]
        t_ref[...] = target
        g_ref[...] = predicted - target


def second(sets, att, logits, idx, row_count, head_count, scale):
    rows, keys = logits.shape
    queries = row_count * head_count
    spans = span_count
    per = rows // row_count
    step_rows = min(8, rows)
    groups = step_rows // row_count
    shape = jax.ShapeDtypeStruct((rows, keys), jnp.float32)

    def mine(i, g):
        return (0, i * groups + g, 0, 0)

    operands, specs, total = [], [], 0
    for e, top, parts in sets:
        total += parts
        for a in (e, top):
            operands.append(a.reshape((parts, per) + a.shape[1:]))
            specs.append(pl.BlockSpec((parts, 1) + a.shape[1:], mine))
    layout = [parts for _, _, parts in sets]
    return pl.pallas_call(
        functools.partial(second_kernel, row_count, head_count, scale, spans, per, layout),
        out_shape=(shape, shape),
        grid=(rows // step_rows, groups),
        in_specs=specs
        + [
            pl.BlockSpec((2, total * per, 1, queries), lambda i, g: (0, 0, 0, 0)),
            pl.BlockSpec((step_rows, keys), lambda i, g: (i, 0)),
            pl.BlockSpec((2, step_rows, lanes), lambda i, g: (0, i, 0)),
        ],
        out_specs=[pl.BlockSpec((step_rows, keys), lambda i, g: (i, 0))] * 2,
        scratch_shapes=[
            pltpu.VMEM((spans, total, queries, lanes), jnp.float32),
            pltpu.VMEM((2, total, queries, lanes), jnp.float32),
            pltpu.VMEM((groups, row_count, keys), jnp.float32),
        ],
        compiler_params=pltpu.CompilerParams(vmem_limit_bytes=second_vmem),
        cost_estimate=pl.CostEstimate(
            flops=2 * total * per * queries * keys,
            bytes_accessed=total * per * queries * keys * 2,
            transcendentals=rows * keys,
        ),
    )(*operands, att[:, :, None, :], logits, idx)


def logits_kernel(row_count, scale, lengths, start, *refs):
    *part_refs, logits_ref, idx_ref = refs
    rows, keys = logits_ref.shape
    per = rows // row_count
    key = lax.broadcasted_iota(jnp.int32, (row_count, keys), 1) + start[0]
    row = lax.broadcasted_iota(jnp.int32, (row_count, keys), 0)
    for i in range(per):
        value = None
        for part in part_refs:
            for p in range(i, part.shape[0], per):
                value = part[p] if value is None else value + part[p]
        length = jnp.full((row_count, keys), lengths[i * row_count], jnp.int32)
        for r in range(1, row_count):
            length = jnp.where(row == r, lengths[i * row_count + r], length)
        value = jnp.where(key < length, value * scale, -jnp.inf)
        logits_ref[i * row_count : (i + 1) * row_count, :] = value
        largest = jnp.maximum(jnp.max(value, axis=1, keepdims=True), far_below)
        rest = jnp.sum(jnp.exp(value - largest), axis=1, keepdims=True)
        idx_ref[0, i * row_count : (i + 1) * row_count, :] = jnp.broadcast_to(largest, (row_count, lanes))
        idx_ref[1, i * row_count : (i + 1) * row_count, :] = jnp.broadcast_to(rest, (row_count, lanes))


def index_logits(parts, lengths, start, scale):
    row_count, keys = parts[0].shape[1:]
    rows = lengths.shape[0]
    scalars = pl.BlockSpec(memory_space=pltpu.SMEM)
    return pl.pallas_call(
        functools.partial(logits_kernel, row_count, scale),
        out_shape=(
            jax.ShapeDtypeStruct((rows, keys), jnp.float32),
            jax.ShapeDtypeStruct((2, rows, lanes), jnp.float32),
        ),
        in_specs=[scalars, scalars] + [pl.BlockSpec(memory_space=pltpu.VMEM)] * len(parts),
        compiler_params=pltpu.CompilerParams(vmem_limit_bytes=32 * 2**20),
    )(lengths, start, *parts)


def swap(x, bit):
    size = lax.axis_size("ctx")
    return lax.ppermute(x, "ctx", [(i, i ^ bit) for i in range(size)])


def bring_and_sweep(block, sweep_blocks):
    ctx, head = lax.axis_size("ctx"), lax.axis_size("head")
    me, plane = lax.axis_index("ctx"), lax.axis_index("head")
    per = ctx // head
    if ctx != 16 or head != 2:
        moves = []
        for c in range(ctx):
            for h in range(head):
                moves.append((c * head + h, (h * per + c % per) * head + c // per))
        held, far, bit = lax.ppermute(block, ("ctx", "head"), moves), [0], 1
        while bit < ctx:
            held = jnp.concatenate([held, swap(held, bit)])
            far = far + [k ^ bit for k in far]
            bit *= 2
        return [sweep_blocks([held], [jnp.bitwise_xor(me, k) for k in far], head)]
    half = ctx // 2
    home = me // half == plane
    mine = lax.rem(me, half)

    def place(distance):
        return mine ^ distance

    to_away, to_beside, to_both = [], [], []
    for c in range(ctx):
        for h in range(head):
            if c // half == h:
                to_away.append((c * head + h, (c ^ half) * head + h))
            else:
                to_beside.append((c * head + h, c * head + (1 - h)))
                to_both.append((c * head + h, (c ^ half) * head + (1 - h)))
    away = lax.ppermute(block, ("ctx", "head"), to_away)
    beside = lax.ppermute(block, ("ctx", "head"), to_beside)
    away_beside = lax.ppermute(block, ("ctx", "head"), to_both)
    one = jnp.where(home, block, away)
    one_x, one_z = swap(one, 2), swap(one, 4)
    two = jnp.where(home, beside, away_beside)
    two_x, two_z = swap(two, 2), swap(two, 4)
    one_zx = swap(one_z, 2)
    two_xz = swap(two_x, 4)
    swept = []
    for part in ([one, one_x, one_z, one_zx], [two, two_x, two_z, two_xz]):
        blocks = part + [swap(a, 1) for a in part]
        swept.append(sweep_blocks(blocks, [place(k) for k in (0, 2, 4, 6, 1, 3, 5, 7)], 1))
    return swept


def body(absorbed_query, index_query, index_weight, kv_cache, index_keys, lengths):
    row_count, head_count, latent = absorbed_query.shape
    idx_heads, idx_width = index_query.shape[1:]
    ctx, head = lax.axis_size("ctx"), lax.axis_size("head")
    keys = kv_cache.shape[0]
    me, plane = lax.axis_index("ctx"), lax.axis_index("head")
    start = jnp.reshape(me * keys, (1,)).astype(jnp.int32)
    per = ctx // head
    own_rows = per * row_count
    own_lengths = lax.dynamic_slice_in_dim(lengths, plane * own_rows, own_rows)

    half = idx_width // 2
    idx_flat = index_query.reshape(row_count * idx_heads, idx_width)
    idx_packed = jnp.concatenate([idx_flat[:, :half], idx_flat[:, half:]])
    query = jnp.concatenate([absorbed_query.reshape(row_count * head_count, latent), idx_packed], axis=1)
    width = latent + half
    weight = index_weight.reshape(1, row_count * idx_heads)
    weight = jnp.pad(weight, ((0, 15), (0, width - weight.shape[1])))
    block = jnp.concatenate([query, weight])[None]

    kv = kv_cache.T

    def sweep_blocks(blocks, places, parts):
        info = jnp.concatenate([start, jnp.stack(places).astype(jnp.int32)] + [own_lengths] * parts)
        return sweep(blocks, info, kv, index_keys, row_count, head_count, idx_heads, latent)

    swept = bring_and_sweep(block, sweep_blocks)
    sets = [(e, top, e.shape[0] // per) for e, top, _, _ in swept]
    stat = jnp.concatenate([stat for _, _, stat, _ in swept])
    queries = row_count * head_count

    logits, idx = index_logits([part for _, _, _, part in swept], own_lengths, start, idx_width ** (-0.5))
    idx_max, idx_total = idx[0, :, 0], idx[1, :, 0]

    largest = jnp.concatenate([stat[:, 0, :].reshape(-1) * attention_scale, idx_max])
    total = jnp.concatenate([stat[:, 1, :].reshape(-1), idx_total])
    state = jnp.stack([largest, total])
    bit = 1
    while bit < ctx:
        other = swap(state, bit)
        top_two = jnp.maximum(state[0], other[0])
        merged = state[1] * jnp.exp(state[0] - top_two) + other[1] * jnp.exp(other[0] - top_two)
        state = jnp.stack([top_two, merged])
        bit *= 2
    whole = float(keys * ctx)
    factor = whole / (levels * head * head_count)
    att = jnp.stack([state[0, : ctx * queries] * (1.0 / attention_scale), factor / state[1, : ctx * queries]])
    att = att.reshape(2, ctx, queries)
    idx = jnp.stack([state[0, ctx * queries :], whole / state[1, ctx * queries :]])
    idx = jnp.broadcast_to(idx[:, :, None], idx.shape + (lanes,))
    return second(sets, att, logits, idx, row_count, head_count, attention_scale * log2_e)


def solution(mesh):
    return jax.shard_map(
        body,
        mesh=mesh,
        in_specs=(
            P("ctx", "head", None),
            P("ctx", "head", None),
            P("ctx", "head"),
            P("ctx", None),
            P("ctx", None),
            P(),
        ),
        out_specs=(P("head", "ctx"), P("head", "ctx")),
        check_vma=False,
    )
```

```python
import functools

import jax
import jax.numpy as jnp
from jax import lax
from jax.experimental import pallas as pl
from jax.experimental.pallas import tpu as pltpu
from jax.sharding import PartitionSpec as P

attention_scale = 192.0 ** (-0.5)
log2_e = 1.4426950408889634
far_below = -1e30
levels = 32767.0
lanes = 128
span_count = 4
lag = 2
vmem_limit = 32 * 2**20
second_vmem = 57 * 2**20


def sweep_kernel(row_count, head_count, idx_heads, latent, spans, pack, sizes, info, kv_ref, ik_ref, *rest):
    sources, rest = rest[: len(sizes)], rest[len(sizes) :]
    e_hbm, top_hbm, stat_ref, part_ref, *rest = rest
    e_slots, top_slots, s_all, m_all, run_m, run_t, turn_m, turn_t, iq_ref, w_ref, q_slots, e_sems, top_sems, q_sems = rest
    count = sum(sizes)
    queries = row_count * head_count
    keys = kv_ref.shape[1]
    span = keys // spans
    idx_queries = row_count * idx_heads
    scale = attention_scale * log2_e
    start = info[0]

    def query_copy(tile, act):
        passed = 0
        for source, size in zip(sources, sizes):

            @pl.when(jnp.logical_and(tile >= passed, tile < passed + size))
            def _(source=source, passed=passed):
                into = lax.rem(tile, 2 * pack)
                act(pltpu.make_async_copy(source.at[tile - passed], q_slots.at[into], q_sems.at[into]))

            passed += size

    def result_copies(tile, act):
        slot, place = lax.rem(tile, 3 * pack), info[1 + tile]
        act(pltpu.make_async_copy(e_slots.at[slot], e_hbm.at[place], e_sems.at[slot]))
        act(pltpu.make_async_copy(top_slots.at[slot], top_hbm.at[place], top_sems.at[slot]))

    def begin(copy):
        copy.start()

    def await_end(copy):
        copy.wait()

    def scores(u, q_ref, first_row, masked):
        s_ref, m_ref = s_all.at[u], m_all.at[u]
        for at in range(0, span, min(256, span)):
            size = min(256, span)
            y = jnp.dot(
                q_ref[:queries, :latent],
                kv_ref[:, u * span + at : u * span + at + size],
                preferred_element_type=jnp.float32,
            )
            if masked:
                key = lax.broadcasted_iota(jnp.int32, (head_count, size), 1) + (start + u * span + at)
                pieces = []
                for r in range(row_count):
                    piece = y[r * head_count : (r + 1) * head_count]
                    pieces.append(jnp.where(key < info[first_row + r], piece, -jnp.inf))
                y = jnp.concatenate(pieces, axis=0)
            s_ref[:, at : at + size] = y
            top = y[:, :lanes]
            for j in range(lanes, size, lanes):
                top = jnp.maximum(top, y[:, j : j + lanes])
            m_ref[...] = jnp.maximum(top, far_below if at == 0 else m_ref[...])

    def index_part(u, q_ref, place):
        if u == 0:
            packed = q_ref[: 2 * idx_queries, latent:]
            iq_ref[...] = jnp.concatenate([packed[:idx_queries], packed[idx_queries:]], axis=1)
            weight = q_ref[queries : queries + 8, :lanes].astype(jnp.float32)[0:1]
            w_ref[...] = jnp.transpose(jnp.broadcast_to(weight, (lanes, lanes)))[:idx_queries]
        for at in range(u * span, (u + 1) * span, min(256, span)):
            size = min(256, span)
            inner = lax.dot_general(
                iq_ref[...], ik_ref[at : at + size, :], (((1,), (1,)), ((), ())), preferred_element_type=jnp.float32
            )
            for j in range(0, size, lanes):
                product = jnp.maximum(inner[:, j : j + lanes], 0.0) * w_ref[...]
                product = jnp.sum(product.reshape(row_count, idx_heads, lanes), axis=1)
                part_ref[place, :, at + j : at + j + lanes] = product

    def exponentials(u, slot):
        s_ref, m_ref = s_all.at[u], m_all.at[u]
        out, top_out = e_slots.at[slot], top_slots.at[slot]
        for q in range(0, queries, 16):
            top = m_ref[q : q + 16, :]
            total = None
            for j in range(0, span, lanes):
                e = jnp.exp2((s_ref[q : q + 16, j : j + lanes] - top) * scale)
                total = e if total is None else total + e
                out[q : q + 16, u * span + j : u * span + j + lanes] = jnp.round(e * levels).astype(jnp.int32).astype(jnp.int16)
            top_out[q : q + 16, u * lanes : (u + 1) * lanes] = top
            if u == 0:
                run_m[q : q + 16, :] = top
                run_t[q : q + 16, :] = total
            else:
                held = run_m[q : q + 16, :]
                larger = jnp.maximum(held, top)
                run_m[q : q + 16, :] = larger
                run_t[q : q + 16, :] = run_t[q : q + 16, :] * jnp.exp2((held - larger) * scale) + total * jnp.exp2(
                    (top - larger) * scale
                )

    def turn():
        turn_m[...] = jnp.transpose(run_m[...])
        turn_t[...] = jnp.transpose(run_t[...])

    def finish(place):
        top = turn_m[...]
        largest = jnp.max(top, axis=0, keepdims=True)
        stat_ref[place, 0:1, :] = largest
        stat_ref[place, 1:2, :] = jnp.sum(turn_t[...] * jnp.exp2((top - largest) * scale), axis=0, keepdims=True)

    def guarded(tile, action):
        pl.when(jnp.logical_and(tile >= 0, tile < count))(action)

    def boundary(i):
        for k in range(pack):
            old, done = pack * (i - 2) - 1 + k, pack * (i - 1) - 1 + k
            guarded(old, functools.partial(result_copies, old, await_end))
            guarded(done, functools.partial(result_copies, done, begin))

    def step(i, _):
        tiles = [i * pack + k for k in range(pack)]
        rows = [1 + count + info[1 + tile] * row_count for tile in tiles]
        shortest = info[rows[0]]
        for first_row in rows:
            for r in range(row_count):
                shortest = jnp.minimum(shortest, info[first_row + r])
        clear = shortest >= start + keys
        for tile in tiles:
            query_copy(tile, await_end)
        for tile in tiles:
            query_copy(tile + pack, begin)
        boundary(i)

        def work(masked):
            for tile, first_row in zip(tiles, rows):
                slot = lax.rem(tile, 3 * pack)
                other = lax.rem(tile + 3 * pack - 1, 3 * pack)
                q_ref = q_slots.at[lax.rem(tile, 2 * pack)]
                place = info[1 + tile]
                before = info[1 + jnp.maximum(tile - 1, 0)]
                for u in range(spans):
                    scores(u, q_ref, first_row, masked)
                    if u == lag:
                        turn()
                    index_part(u, q_ref, place)
                    exponentials((u - lag) % spans, other if u < lag else slot)
                    if u == min(lag + 1, spans - 1):
                        finish(before)

        pl.when(clear)(lambda: work(False))
        pl.when(jnp.logical_not(clear))(lambda: work(True))
        return 0

    steps = count // pack
    for tile in range(pack):
        query_copy(tile, begin)
    lax.fori_loop(0, steps, step, 0)
    boundary(steps)
    for u in range(spans - lag, spans):
        exponentials(u, (count - 1) % (3 * pack))
    result_copies(count - 1, begin)
    turn()
    finish(info[count])
    for tile in range(max(0, count - 1 - pack), count):
        result_copies(tile, await_end)


def sweep(blocks, info, kv, idx_keys, row_count, head_count, idx_heads, latent):
    sizes = [a.shape[0] for a in blocks]
    count = sum(sizes)
    block_rows, width = blocks[0].shape[1:]
    keys = kv.shape[1]
    queries = row_count * head_count
    spans = span_count
    span = keys // spans
    pack = 1
    kernel = functools.partial(sweep_kernel, row_count, head_count, idx_heads, latent, spans, pack, sizes)
    whole = pl.BlockSpec(memory_space=pltpu.VMEM)
    far = pl.BlockSpec(memory_space=pltpu.HBM)
    return pl.pallas_call(
        kernel,
        out_shape=(
            pltpu.HBM((count, queries, keys), jnp.int16),
            pltpu.HBM((count, queries, spans * lanes), jnp.float32),
            jax.ShapeDtypeStruct((count, 2, queries), jnp.float32),
            jax.ShapeDtypeStruct((count, row_count, keys), jnp.float32),
        ),
        in_specs=[pl.BlockSpec(memory_space=pltpu.SMEM), whole, whole] + [far] * len(blocks),
        out_specs=[far, far, whole, whole],
        scratch_shapes=[
            pltpu.VMEM((3 * pack, queries, keys), jnp.int16),
            pltpu.VMEM((3 * pack, queries, spans * lanes), jnp.float32),
        ]
        + [pltpu.VMEM((spans, queries, span), jnp.float32), pltpu.VMEM((spans, queries, lanes), jnp.float32)]
        + [pltpu.VMEM((queries, lanes), jnp.float32)] * 2
        + [pltpu.VMEM((lanes, queries), jnp.float32)] * 2
        + [pltpu.VMEM((row_count * idx_heads, idx_keys.shape[1]), jnp.bfloat16)]
        + [pltpu.VMEM((row_count * idx_heads, lanes), jnp.float32)]
        + [pltpu.VMEM((2 * pack, block_rows, width), jnp.bfloat16)]
        + [pltpu.SemaphoreType.DMA((3 * pack,))] * 2
        + [pltpu.SemaphoreType.DMA((2 * pack,))],
        compiler_params=pltpu.CompilerParams(vmem_limit_bytes=vmem_limit),
        cost_estimate=pl.CostEstimate(
            flops=2 * count * queries * keys * 1024,
            bytes_accessed=count * queries * keys * 2,
            transcendentals=count * queries * keys,
        ),
    )(info, kv, idx_keys, *blocks)


def second_kernel(row_count, head_count, scale, spans, per, layout, *refs):
    arrays, refs = refs[: 2 * len(layout)], refs[2 * len(layout) :]
    att_ref, logits_ref, idx_ref, t_ref, g_ref, c_ref, turn_ref, sum_ref = refs
    queries = c_ref.shape[2]
    keys = t_ref.shape[1]
    span = keys // spans
    groups = t_ref.shape[0] // row_count
    group = pl.program_id(1)
    first = pl.program_id(0) * groups + group

    members = []
    for k, parts in enumerate(layout):
        for p in range(parts):
            members.append((len(members) * per + first, arrays[2 * k].at[p, 0], arrays[2 * k + 1].at[p, 0]))

    for p, (place, _, _) in enumerate(members):
        turn_ref[0, p] = jnp.transpose(jnp.broadcast_to(att_ref[0, place], (lanes, queries)))
        turn_ref[1, p] = jnp.transpose(jnp.broadcast_to(att_ref[1, place], (lanes, queries)))

    def factors(u):
        for p, (_, _, top) in enumerate(members):
            top_u = top[:, u * lanes : (u + 1) * lanes]
            c_ref[u, p] = jnp.exp2((top_u - turn_ref[0, p]) * scale) * turn_ref[1, p]

    factors(0)
    for u in range(spans):
        if u + 1 < spans:
            factors(u + 1)
        for r in range(row_count):
            acc = [None] * (span // lanes)
            for p, (_, source, _) in enumerate(members):
                for q in range(r * head_count, (r + 1) * head_count, 16):
                    c = c_ref[u, p, q : q + 16, :]
                    for k in range(len(acc)):
                        at = u * span + k * lanes
                        term = source[q : q + 16, at : at + lanes].astype(jnp.float32) * c
                        term = term[:8] + term[8:]
                        acc[k] = term if acc[k] is None else acc[k] + term
            for k in range(len(acc)):
                at = u * span + k * lanes
                sum_ref[group, r : r + 1, at : at + lanes] = jnp.sum(acc[k], axis=0, keepdims=True)

    @pl.when(group == groups - 1)
    def _():
        target = jnp.concatenate([sum_ref[g] for g in range(groups)], axis=0)
        predicted = jnp.exp(logits_ref[...] - idx_ref[0, :, 0:1]) * idx_ref[1, :, 0:1]
        t_ref[...] = target
        g_ref[...] = predicted - target


def second(sets, att, logits, idx, row_count, head_count, scale):
    rows, keys = logits.shape
    queries = row_count * head_count
    spans = span_count
    per = rows // row_count
    step_rows = min(8, rows)
    groups = step_rows // row_count
    shape = jax.ShapeDtypeStruct((rows, keys), jnp.float32)

    def mine(i, g):
        return (0, i * groups + g, 0, 0)

    operands, specs, total = [], [], 0
    for e, top, parts in sets:
        total += parts
        for a in (e, top):
            operands.append(a.reshape((parts, per) + a.shape[1:]))
            specs.append(pl.BlockSpec((parts, 1) + a.shape[1:], mine))
    layout = [parts for _, _, parts in sets]
    return pl.pallas_call(
        functools.partial(second_kernel, row_count, head_count, scale, spans, per, layout),
        out_shape=(shape, shape),
        grid=(rows // step_rows, groups),
        in_specs=specs
        + [
            pl.BlockSpec((2, total * per, 1, queries), lambda i, g: (0, 0, 0, 0)),
            pl.BlockSpec((step_rows, keys), lambda i, g: (i, 0)),
            pl.BlockSpec((2, step_rows, lanes), lambda i, g: (0, i, 0)),
        ],
        out_specs=[pl.BlockSpec((step_rows, keys), lambda i, g: (i, 0))] * 2,
        scratch_shapes=[
            pltpu.VMEM((spans, total, queries, lanes), jnp.float32),
            pltpu.VMEM((2, total, queries, lanes), jnp.float32),
            pltpu.VMEM((groups, row_count, keys), jnp.float32),
        ],
        compiler_params=pltpu.CompilerParams(vmem_limit_bytes=second_vmem),
        cost_estimate=pl.CostEstimate(
            flops=2 * total * per * queries * keys,
            bytes_accessed=total * per * queries * keys * 2,
            transcendentals=rows * keys,
        ),
    )(*operands, att[:, :, None, :], logits, idx)


def logits_kernel(row_count, scale, lengths, start, *refs):
    *part_refs, logits_ref, idx_ref = refs
    rows, keys = logits_ref.shape
    per = rows // row_count
    key = lax.broadcasted_iota(jnp.int32, (row_count, keys), 1) + start[0]
    row = lax.broadcasted_iota(jnp.int32, (row_count, keys), 0)
    for i in range(per):
        value = None
        for part in part_refs:
            for p in range(i, part.shape[0], per):
                value = part[p] if value is None else value + part[p]
        length = jnp.full((row_count, keys), lengths[i * row_count], jnp.int32)
        for r in range(1, row_count):
            length = jnp.where(row == r, lengths[i * row_count + r], length)
        value = jnp.where(key < length, value * scale, -jnp.inf)
        logits_ref[i * row_count : (i + 1) * row_count, :] = value
        largest = jnp.maximum(jnp.max(value, axis=1, keepdims=True), far_below)
        rest = jnp.sum(jnp.exp(value - largest), axis=1, keepdims=True)
        idx_ref[0, i * row_count : (i + 1) * row_count, :] = jnp.broadcast_to(largest, (row_count, lanes))
        idx_ref[1, i * row_count : (i + 1) * row_count, :] = jnp.broadcast_to(rest, (row_count, lanes))


def index_logits(parts, lengths, start, scale):
    row_count, keys = parts[0].shape[1:]
    rows = lengths.shape[0]
    scalars = pl.BlockSpec(memory_space=pltpu.SMEM)
    return pl.pallas_call(
        functools.partial(logits_kernel, row_count, scale),
        out_shape=(
            jax.ShapeDtypeStruct((rows, keys), jnp.float32),
            jax.ShapeDtypeStruct((2, rows, lanes), jnp.float32),
        ),
        in_specs=[scalars, scalars] + [pl.BlockSpec(memory_space=pltpu.VMEM)] * len(parts),
        compiler_params=pltpu.CompilerParams(vmem_limit_bytes=32 * 2**20),
    )(lengths, start, *parts)


def swap(x, bit):
    size = lax.axis_size("ctx")
    return lax.ppermute(x, "ctx", [(i, i ^ bit) for i in range(size)])


def bring_and_sweep(block, sweep_blocks):
    ctx, head = lax.axis_size("ctx"), lax.axis_size("head")
    me, plane = lax.axis_index("ctx"), lax.axis_index("head")
    per = ctx // head
    if ctx != 16 or head != 2:
        moves = []
        for c in range(ctx):
            for h in range(head):
                moves.append((c * head + h, (h * per + c % per) * head + c // per))
        held, far, bit = lax.ppermute(block, ("ctx", "head"), moves), [0], 1
        while bit < ctx:
            held = jnp.concatenate([held, swap(held, bit)])
            far = far + [k ^ bit for k in far]
            bit *= 2
        return [sweep_blocks([held], [jnp.bitwise_xor(me, k) for k in far], head)]
    half = ctx // 2
    home = me // half == plane
    mine = lax.rem(me, half)

    def place(other, distance):
        return (plane ^ other) * half + (mine ^ distance)

    to_away, to_beside, to_both = [], [], []
    for c in range(ctx):
        for h in range(head):
            if c // half == h:
                to_away.append((c * head + h, (c ^ half) * head + h))
            else:
                to_beside.append((c * head + h, c * head + (1 - h)))
                to_both.append((c * head + h, (c ^ half) * head + (1 - h)))
    away = lax.ppermute(block, ("ctx", "head"), to_away)
    beside = lax.ppermute(block, ("ctx", "head"), to_beside)
    away_beside = lax.ppermute(block, ("ctx", "head"), to_both)
    one = jnp.where(home, block, away)
    one_x, one_z = swap(one, 2), swap(one, 4)
    two = jnp.where(home, beside, away_beside)
    two_x, two_z = swap(two, 2), swap(two, 4)
    one_zx = swap(one_z, 2)
    two_xz = swap(two_x, 4)
    blocks, places = [], []
    for other, part in enumerate(([one, one_x, one_z, one_zx], [two, two_x, two_z, two_xz])):
        blocks += part + [swap(a, 1) for a in part]
        places += [place(other, k) for k in (0, 2, 4, 6, 1, 3, 5, 7)]
    return [sweep_blocks(blocks, places, head)]


def body(absorbed_query, index_query, index_weight, kv_cache, index_keys, lengths):
    row_count, head_count, latent = absorbed_query.shape
    idx_heads, idx_width = index_query.shape[1:]
    ctx, head = lax.axis_size("ctx"), lax.axis_size("head")
    keys = kv_cache.shape[0]
    me, plane = lax.axis_index("ctx"), lax.axis_index("head")
    start = jnp.reshape(me * keys, (1,)).astype(jnp.int32)
    per = ctx // head
    own_rows = per * row_count
    own_lengths = lax.dynamic_slice_in_dim(lengths, plane * own_rows, own_rows)

    half = idx_width // 2
    idx_flat = index_query.reshape(row_count * idx_heads, idx_width)
    idx_packed = jnp.concatenate([idx_flat[:, :half], idx_flat[:, half:]])
    query = jnp.concatenate([absorbed_query.reshape(row_count * head_count, latent), idx_packed], axis=1)
    width = latent + half
    weight = index_weight.reshape(1, row_count * idx_heads)
    weight = jnp.pad(weight, ((0, 15), (0, width - weight.shape[1])))
    block = jnp.concatenate([query, weight])[None]

    kv = kv_cache.T

    def sweep_blocks(blocks, places, parts):
        info = jnp.concatenate([start, jnp.stack(places).astype(jnp.int32)] + [own_lengths] * parts)
        return sweep(blocks, info, kv, index_keys, row_count, head_count, idx_heads, latent)

    swept = bring_and_sweep(block, sweep_blocks)
    sets = [(e, top, e.shape[0] // per) for e, top, _, _ in swept]
    stat = jnp.concatenate([stat for _, _, stat, _ in swept])
    queries = row_count * head_count

    logits, idx = index_logits([part for _, _, _, part in swept], own_lengths, start, idx_width ** (-0.5))
    idx_max, idx_total = idx[0, :, 0], idx[1, :, 0]

    largest = jnp.concatenate([stat[:, 0, :].reshape(-1) * attention_scale, idx_max])
    total = jnp.concatenate([stat[:, 1, :].reshape(-1), idx_total])
    state = jnp.stack([largest, total])
    bit = 1
    while bit < ctx:
        other = swap(state, bit)
        top_two = jnp.maximum(state[0], other[0])
        merged = state[1] * jnp.exp(state[0] - top_two) + other[1] * jnp.exp(other[0] - top_two)
        state = jnp.stack([top_two, merged])
        bit *= 2
    whole = float(keys * ctx)
    factor = whole / (levels * head * head_count)
    att = jnp.stack([state[0, : ctx * queries] * (1.0 / attention_scale), factor / state[1, : ctx * queries]])
    att = att.reshape(2, ctx, queries)
    idx = jnp.stack([state[0, ctx * queries :], whole / state[1, ctx * queries :]])
    idx = jnp.broadcast_to(idx[:, :, None], idx.shape + (lanes,))
    return second(sets, att, logits, idx, row_count, head_count, attention_scale * log2_e)


def solution(mesh):
    return jax.shard_map(
        body,
        mesh=mesh,
        in_specs=(
            P("ctx", "head", None),
            P("ctx", "head", None),
            P("ctx", "head"),
            P("ctx", None),
            P("ctx", None),
            P(),
        ),
        out_specs=(P("head", "ctx"), P("head", "ctx")),
        check_vma=False,
    )
```

```python
import functools

import jax
import jax.numpy as jnp
from jax import lax
from jax.experimental import pallas as pl
from jax.experimental.pallas import tpu as pltpu
from jax.sharding import PartitionSpec as P

attention_scale = 192.0 ** (-0.5)
log2_e = 1.4426950408889634
far_below = -1e30
levels = 32767.0
lanes = 128
span_count = 4
lag = 2
vmem_limit = 32 * 2**20
second_vmem = 57 * 2**20


def sweep_kernel(row_count, head_count, idx_heads, latent, spans, pack, sizes, info, kv_hbm, ik_hbm, *rest):
    sources, rest = rest[: len(sizes)], rest[len(sizes) :]
    e_hbm, top_hbm, stat_ref, part_ref, *rest = rest
    e_slots, top_slots, s_all, m_all, run_m, run_t, turn_m, turn_t, iq_ref, w_ref, q_slots, kv_ref, ik_ref, e_sems, top_sems, q_sems, key_sems = rest
    count = sum(sizes)
    queries = row_count * head_count
    keys = kv_hbm.shape[1]
    span = keys // spans
    idx_queries = row_count * idx_heads
    scale = attention_scale * log2_e
    start = info[0]

    def query_copy(tile, act):
        passed = 0
        for source, size in zip(sources, sizes):

            @pl.when(jnp.logical_and(tile >= passed, tile < passed + size))
            def _(source=source, passed=passed):
                into = lax.rem(tile, 2 * pack)
                act(pltpu.make_async_copy(source.at[tile - passed], q_slots.at[into], q_sems.at[into]))

            passed += size

    def result_copies(tile, act):
        slot, place = lax.rem(tile, 3 * pack), info[1 + tile]
        act(pltpu.make_async_copy(e_slots.at[slot], e_hbm.at[place], e_sems.at[slot]))
        act(pltpu.make_async_copy(top_slots.at[slot], top_hbm.at[place], top_sems.at[slot]))

    def begin(copy):
        copy.start()

    def await_end(copy):
        copy.wait()

    def scores(u, q_ref, first_row, masked):
        s_ref, m_ref = s_all.at[u], m_all.at[u]
        for at in range(0, span, min(256, span)):
            size = min(256, span)
            y = jnp.dot(
                q_ref[:queries, :latent],
                kv_ref[:, u * span + at : u * span + at + size],
                preferred_element_type=jnp.float32,
            )
            if masked:
                key = lax.broadcasted_iota(jnp.int32, (head_count, size), 1) + (start + u * span + at)
                pieces = []
                for r in range(row_count):
                    piece = y[r * head_count : (r + 1) * head_count]
                    pieces.append(jnp.where(key < info[first_row + r], piece, -jnp.inf))
                y = jnp.concatenate(pieces, axis=0)
            s_ref[:, at : at + size] = y
            top = y[:, :lanes]
            for j in range(lanes, size, lanes):
                top = jnp.maximum(top, y[:, j : j + lanes])
            m_ref[...] = jnp.maximum(top, far_below if at == 0 else m_ref[...])

    def index_part(u, q_ref, place):
        if u == 0:
            packed = q_ref[: 2 * idx_queries, latent:]
            iq_ref[...] = jnp.concatenate([packed[:idx_queries], packed[idx_queries:]], axis=1)
            weight = q_ref[queries : queries + 8, :lanes].astype(jnp.float32)[0:1]
            w_ref[...] = jnp.transpose(jnp.broadcast_to(weight, (lanes, lanes)))[:idx_queries]
        for at in range(u * span, (u + 1) * span, min(256, span)):
            size = min(256, span)
            inner = lax.dot_general(
                iq_ref[...], ik_ref[at : at + size, :], (((1,), (1,)), ((), ())), preferred_element_type=jnp.float32
            )
            for j in range(0, size, lanes):
                product = jnp.maximum(inner[:, j : j + lanes], 0.0) * w_ref[...]
                product = jnp.sum(product.reshape(row_count, idx_heads, lanes), axis=1)
                part_ref[place, :, at + j : at + j + lanes] = product

    def exponentials(u, slot):
        s_ref, m_ref = s_all.at[u], m_all.at[u]
        out, top_out = e_slots.at[slot], top_slots.at[slot]
        for q in range(0, queries, 16):
            top = m_ref[q : q + 16, :]
            total = None
            for j in range(0, span, lanes):
                e = jnp.exp2((s_ref[q : q + 16, j : j + lanes] - top) * scale)
                total = e if total is None else total + e
                out[q : q + 16, u * span + j : u * span + j + lanes] = jnp.round(e * levels).astype(jnp.int32).astype(jnp.int16)
            top_out[q : q + 16, u * lanes : (u + 1) * lanes] = top
            if u == 0:
                run_m[q : q + 16, :] = top
                run_t[q : q + 16, :] = total
            else:
                held = run_m[q : q + 16, :]
                larger = jnp.maximum(held, top)
                run_m[q : q + 16, :] = larger
                run_t[q : q + 16, :] = run_t[q : q + 16, :] * jnp.exp2((held - larger) * scale) + total * jnp.exp2(
                    (top - larger) * scale
                )

    def turn():
        turn_m[...] = jnp.transpose(run_m[...])
        turn_t[...] = jnp.transpose(run_t[...])

    def finish(place):
        top = turn_m[...]
        largest = jnp.max(top, axis=0, keepdims=True)
        stat_ref[place, 0:1, :] = largest
        stat_ref[place, 1:2, :] = jnp.sum(turn_t[...] * jnp.exp2((top - largest) * scale), axis=0, keepdims=True)

    def guarded(tile, action):
        pl.when(jnp.logical_and(tile >= 0, tile < count))(action)

    def boundary(i):
        for k in range(pack):
            old, done = pack * (i - 2) - 1 + k, pack * (i - 1) - 1 + k
            guarded(old, functools.partial(result_copies, old, await_end))
            guarded(done, functools.partial(result_copies, done, begin))

    def step(i, _):
        tiles = [i * pack + k for k in range(pack)]
        rows = [1 + count + info[1 + tile] * row_count for tile in tiles]
        shortest = info[rows[0]]
        for first_row in rows:
            for r in range(row_count):
                shortest = jnp.minimum(shortest, info[first_row + r])
        clear = shortest >= start + keys
        for tile in tiles:
            query_copy(tile, await_end)
        for tile in tiles:
            query_copy(tile + pack, begin)
        boundary(i)

        def work(masked):
            for tile, first_row in zip(tiles, rows):
                slot = lax.rem(tile, 3 * pack)
                other = lax.rem(tile + 3 * pack - 1, 3 * pack)
                q_ref = q_slots.at[lax.rem(tile, 2 * pack)]
                place = info[1 + tile]
                before = info[1 + jnp.maximum(tile - 1, 0)]
                for u in range(spans):
                    scores(u, q_ref, first_row, masked)
                    if u == lag:
                        turn()
                    index_part(u, q_ref, place)
                    exponentials((u - lag) % spans, other if u < lag else slot)
                    if u == min(lag + 1, spans - 1):
                        finish(before)

        pl.when(clear)(lambda: work(False))
        pl.when(jnp.logical_not(clear))(lambda: work(True))
        return 0

    steps = count // pack
    for tile in range(pack):
        query_copy(tile, begin)
    key_copies = []
    for u in range(spans):
        part = pl.ds(u * span, span)
        key_copies.append(pltpu.make_async_copy(kv_hbm.at[:, part], kv_ref.at[:, part], key_sems.at[0, u]))
        key_copies.append(pltpu.make_async_copy(ik_hbm.at[part, :], ik_ref.at[part, :], key_sems.at[1, u]))
    for copy in key_copies:
        copy.start()
    for copy in key_copies:
        copy.wait()
    lax.fori_loop(0, steps, step, 0)
    boundary(steps)
    for u in range(spans - lag, spans):
        exponentials(u, (count - 1) % (3 * pack))
    result_copies(count - 1, begin)
    turn()
    finish(info[count])
    for tile in range(max(0, count - 1 - pack), count):
        result_copies(tile, await_end)


def sweep(blocks, info, kv, idx_keys, row_count, head_count, idx_heads, latent):
    sizes = [a.shape[0] for a in blocks]
    count = sum(sizes)
    block_rows, width = blocks[0].shape[1:]
    keys = kv.shape[1]
    queries = row_count * head_count
    spans = span_count
    span = keys // spans
    pack = 1
    kernel = functools.partial(sweep_kernel, row_count, head_count, idx_heads, latent, spans, pack, sizes)
    whole = pl.BlockSpec(memory_space=pltpu.VMEM)
    far = pl.BlockSpec(memory_space=pltpu.HBM)
    return pl.pallas_call(
        kernel,
        out_shape=(
            pltpu.HBM((count, queries, keys), jnp.int16),
            pltpu.HBM((count, queries, spans * lanes), jnp.float32),
            jax.ShapeDtypeStruct((count, 2, queries), jnp.float32),
            jax.ShapeDtypeStruct((count, row_count, keys), jnp.float32),
        ),
        in_specs=[pl.BlockSpec(memory_space=pltpu.SMEM)] + [far] * (2 + len(blocks)),
        out_specs=[far, far, whole, whole],
        scratch_shapes=[
            pltpu.VMEM((3 * pack, queries, keys), jnp.int16),
            pltpu.VMEM((3 * pack, queries, spans * lanes), jnp.float32),
        ]
        + [pltpu.VMEM((spans, queries, span), jnp.float32), pltpu.VMEM((spans, queries, lanes), jnp.float32)]
        + [pltpu.VMEM((queries, lanes), jnp.float32)] * 2
        + [pltpu.VMEM((lanes, queries), jnp.float32)] * 2
        + [pltpu.VMEM((row_count * idx_heads, idx_keys.shape[1]), jnp.bfloat16)]
        + [pltpu.VMEM((row_count * idx_heads, lanes), jnp.float32)]
        + [pltpu.VMEM((2 * pack, block_rows, width), jnp.bfloat16)]
        + [pltpu.VMEM(kv.shape, jnp.bfloat16), pltpu.VMEM(idx_keys.shape, jnp.bfloat16)]
        + [pltpu.SemaphoreType.DMA((3 * pack,))] * 2
        + [pltpu.SemaphoreType.DMA((2 * pack,)), pltpu.SemaphoreType.DMA((2, spans))],
        compiler_params=pltpu.CompilerParams(vmem_limit_bytes=vmem_limit),
        cost_estimate=pl.CostEstimate(
            flops=2 * count * queries * keys * 1024,
            bytes_accessed=count * queries * keys * 2,
            transcendentals=count * queries * keys,
        ),
    )(info, kv, idx_keys, *blocks)


def second_kernel(row_count, head_count, scale, spans, per, layout, *refs):
    arrays, refs = refs[: 2 * len(layout)], refs[2 * len(layout) :]
    att_ref, logits_ref, idx_ref, t_ref, g_ref, c_ref, turn_ref, sum_ref = refs
    queries = c_ref.shape[2]
    keys = t_ref.shape[1]
    span = keys // spans
    groups = t_ref.shape[0] // row_count
    group = pl.program_id(1)
    first = pl.program_id(0) * groups + group

    members = []
    for k, parts in enumerate(layout):
        for p in range(parts):
            members.append((len(members) * per + first, arrays[2 * k].at[p, 0], arrays[2 * k + 1].at[p, 0]))

    for p, (place, _, _) in enumerate(members):
        turn_ref[0, p] = jnp.transpose(jnp.broadcast_to(att_ref[0, place], (lanes, queries)))
        turn_ref[1, p] = jnp.transpose(jnp.broadcast_to(att_ref[1, place], (lanes, queries)))

    def factors(u):
        for p, (_, _, top) in enumerate(members):
            top_u = top[:, u * lanes : (u + 1) * lanes]
            c_ref[u, p] = jnp.exp2((top_u - turn_ref[0, p]) * scale) * turn_ref[1, p]

    factors(0)
    for u in range(spans):
        if u + 1 < spans:
            factors(u + 1)
        for r in range(row_count):
            acc = [None] * (span // lanes)
            for p, (_, source, _) in enumerate(members):
                for q in range(r * head_count, (r + 1) * head_count, 16):
                    c = c_ref[u, p, q : q + 16, :]
                    for k in range(len(acc)):
                        at = u * span + k * lanes
                        term = source[q : q + 16, at : at + lanes].astype(jnp.float32) * c
                        term = term[:8] + term[8:]
                        acc[k] = term if acc[k] is None else acc[k] + term
            for k in range(len(acc)):
                at = u * span + k * lanes
                sum_ref[group, r : r + 1, at : at + lanes] = jnp.sum(acc[k], axis=0, keepdims=True)

    @pl.when(group == groups - 1)
    def _():
        target = jnp.concatenate([sum_ref[g] for g in range(groups)], axis=0)
        predicted = jnp.exp(logits_ref[...] - idx_ref[0, :, 0:1]) * idx_ref[1, :, 0:1]
        t_ref[...] = target
        g_ref[...] = predicted - target


def second(sets, att, logits, idx, row_count, head_count, scale):
    rows, keys = logits.shape
    queries = row_count * head_count
    spans = span_count
    per = rows // row_count
    step_rows = min(8, rows)
    groups = step_rows // row_count
    shape = jax.ShapeDtypeStruct((rows, keys), jnp.float32)

    def mine(i, g):
        return (0, i * groups + g, 0, 0)

    operands, specs, total = [], [], 0
    for e, top, parts in sets:
        total += parts
        for a in (e, top):
            operands.append(a.reshape((parts, per) + a.shape[1:]))
            specs.append(pl.BlockSpec((parts, 1) + a.shape[1:], mine))
    layout = [parts for _, _, parts in sets]
    return pl.pallas_call(
        functools.partial(second_kernel, row_count, head_count, scale, spans, per, layout),
        out_shape=(shape, shape),
        grid=(rows // step_rows, groups),
        in_specs=specs
        + [
            pl.BlockSpec((2, total * per, 1, queries), lambda i, g: (0, 0, 0, 0)),
            pl.BlockSpec((step_rows, keys), lambda i, g: (i, 0)),
            pl.BlockSpec((2, step_rows, lanes), lambda i, g: (0, i, 0)),
        ],
        out_specs=[pl.BlockSpec((step_rows, keys), lambda i, g: (i, 0))] * 2,
        scratch_shapes=[
            pltpu.VMEM((spans, total, queries, lanes), jnp.float32),
            pltpu.VMEM((2, total, queries, lanes), jnp.float32),
            pltpu.VMEM((groups, row_count, keys), jnp.float32),
        ],
        compiler_params=pltpu.CompilerParams(vmem_limit_bytes=second_vmem),
        cost_estimate=pl.CostEstimate(
            flops=2 * total * per * queries * keys,
            bytes_accessed=total * per * queries * keys * 2,
            transcendentals=rows * keys,
        ),
    )(*operands, att[:, :, None, :], logits, idx)


def logits_kernel(row_count, scale, lengths, start, *refs):
    *part_refs, logits_ref, idx_ref = refs
    rows, keys = logits_ref.shape
    per = rows // row_count
    key = lax.broadcasted_iota(jnp.int32, (row_count, keys), 1) + start[0]
    row = lax.broadcasted_iota(jnp.int32, (row_count, keys), 0)
    for i in range(per):
        value = None
        for part in part_refs:
            for p in range(i, part.shape[0], per):
                value = part[p] if value is None else value + part[p]
        length = jnp.full((row_count, keys), lengths[i * row_count], jnp.int32)
        for r in range(1, row_count):
            length = jnp.where(row == r, lengths[i * row_count + r], length)
        value = jnp.where(key < length, value * scale, -jnp.inf)
        logits_ref[i * row_count : (i + 1) * row_count, :] = value
        largest = jnp.maximum(jnp.max(value, axis=1, keepdims=True), far_below)
        rest = jnp.sum(jnp.exp(value - largest), axis=1, keepdims=True)
        idx_ref[0, i * row_count : (i + 1) * row_count, :] = jnp.broadcast_to(largest, (row_count, lanes))
        idx_ref[1, i * row_count : (i + 1) * row_count, :] = jnp.broadcast_to(rest, (row_count, lanes))


def index_logits(parts, lengths, start, scale):
    row_count, keys = parts[0].shape[1:]
    rows = lengths.shape[0]
    scalars = pl.BlockSpec(memory_space=pltpu.SMEM)
    return pl.pallas_call(
        functools.partial(logits_kernel, row_count, scale),
        out_shape=(
            jax.ShapeDtypeStruct((rows, keys), jnp.float32),
            jax.ShapeDtypeStruct((2, rows, lanes), jnp.float32),
        ),
        in_specs=[scalars, scalars] + [pl.BlockSpec(memory_space=pltpu.VMEM)] * len(parts),
        compiler_params=pltpu.CompilerParams(vmem_limit_bytes=32 * 2**20),
    )(lengths, start, *parts)


def swap(x, bit):
    size = lax.axis_size("ctx")
    return lax.ppermute(x, "ctx", [(i, i ^ bit) for i in range(size)])


def bring_and_sweep(block, sweep_blocks):
    ctx, head = lax.axis_size("ctx"), lax.axis_size("head")
    me, plane = lax.axis_index("ctx"), lax.axis_index("head")
    per = ctx // head
    if ctx != 16 or head != 2:
        moves = []
        for c in range(ctx):
            for h in range(head):
                moves.append((c * head + h, (h * per + c % per) * head + c // per))
        held, far, bit = lax.ppermute(block, ("ctx", "head"), moves), [0], 1
        while bit < ctx:
            held = jnp.concatenate([held, swap(held, bit)])
            far = far + [k ^ bit for k in far]
            bit *= 2
        return [sweep_blocks([held], [jnp.bitwise_xor(me, k) for k in far], head)]
    half = ctx // 2
    home = me // half == plane
    mine = lax.rem(me, half)

    def place(other, distance):
        return (plane ^ other) * half + (mine ^ distance)

    to_away, to_beside, to_both = [], [], []
    for c in range(ctx):
        for h in range(head):
            if c // half == h:
                to_away.append((c * head + h, (c ^ half) * head + h))
            else:
                to_beside.append((c * head + h, c * head + (1 - h)))
                to_both.append((c * head + h, (c ^ half) * head + (1 - h)))
    away = lax.ppermute(block, ("ctx", "head"), to_away)
    beside = lax.ppermute(block, ("ctx", "head"), to_beside)
    away_beside = lax.ppermute(block, ("ctx", "head"), to_both)
    one = jnp.where(home, block, away)
    one_x, one_z = swap(one, 2), swap(one, 4)
    two = jnp.where(home, beside, away_beside)
    two_x, two_z = swap(two, 2), swap(two, 4)
    one_zx = swap(one_z, 2)
    two_xz = swap(two_x, 4)
    blocks, places = [], []
    for other, part in enumerate(([one, one_x, one_z, one_zx], [two, two_x, two_z, two_xz])):
        blocks += part + [swap(a, 1) for a in part]
        places += [place(other, k) for k in (0, 2, 4, 6, 1, 3, 5, 7)]
    return [sweep_blocks(blocks, places, head)]


def body(absorbed_query, index_query, index_weight, kv_cache, index_keys, lengths):
    row_count, head_count, latent = absorbed_query.shape
    idx_heads, idx_width = index_query.shape[1:]
    ctx, head = lax.axis_size("ctx"), lax.axis_size("head")
    keys = kv_cache.shape[0]
    me, plane = lax.axis_index("ctx"), lax.axis_index("head")
    start = jnp.reshape(me * keys, (1,)).astype(jnp.int32)
    per = ctx // head
    own_rows = per * row_count
    own_lengths = lax.dynamic_slice_in_dim(lengths, plane * own_rows, own_rows)

    half = idx_width // 2
    idx_flat = index_query.reshape(row_count * idx_heads, idx_width)
    idx_packed = jnp.concatenate([idx_flat[:, :half], idx_flat[:, half:]])
    query = jnp.concatenate([absorbed_query.reshape(row_count * head_count, latent), idx_packed], axis=1)
    width = latent + half
    weight = index_weight.reshape(1, row_count * idx_heads)
    weight = jnp.pad(weight, ((0, 15), (0, width - weight.shape[1])))
    block = jnp.concatenate([query, weight])[None]

    kv = kv_cache.T

    def sweep_blocks(blocks, places, parts):
        info = jnp.concatenate([start, jnp.stack(places).astype(jnp.int32)] + [own_lengths] * parts)
        return sweep(blocks, info, kv, index_keys, row_count, head_count, idx_heads, latent)

    swept = bring_and_sweep(block, sweep_blocks)
    sets = [(e, top, e.shape[0] // per) for e, top, _, _ in swept]
    stat = jnp.concatenate([stat for _, _, stat, _ in swept])
    queries = row_count * head_count

    logits, idx = index_logits([part for _, _, _, part in swept], own_lengths, start, idx_width ** (-0.5))
    idx_max, idx_total = idx[0, :, 0], idx[1, :, 0]

    largest = jnp.concatenate([stat[:, 0, :].reshape(-1) * attention_scale, idx_max])
    total = jnp.concatenate([stat[:, 1, :].reshape(-1), idx_total])
    state = jnp.stack([largest, total])
    bit = 1
    while bit < ctx:
        other = swap(state, bit)
        top_two = jnp.maximum(state[0], other[0])
        merged = state[1] * jnp.exp(state[0] - top_two) + other[1] * jnp.exp(other[0] - top_two)
        state = jnp.stack([top_two, merged])
        bit *= 2
    whole = float(keys * ctx)
    factor = whole / (levels * head * head_count)
    att = jnp.stack([state[0, : ctx * queries] * (1.0 / attention_scale), factor / state[1, : ctx * queries]])
    att = att.reshape(2, ctx, queries)
    idx = jnp.stack([state[0, ctx * queries :], whole / state[1, ctx * queries :]])
    idx = jnp.broadcast_to(idx[:, :, None], idx.shape + (lanes,))
    return second(sets, att, logits, idx, row_count, head_count, attention_scale * log2_e)


def solution(mesh):
    return jax.shard_map(
        body,
        mesh=mesh,
        in_specs=(
            P("ctx", "head", None),
            P("ctx", "head", None),
            P("ctx", "head"),
            P("ctx", None),
            P("ctx", None),
            P(),
        ),
        out_specs=(P("head", "ctx"), P("head", "ctx")),
        check_vma=False,
    )
```
